512 devices in a mesh: tm: 32 (over x_lo, y, core), height: 8 (over z), rep: 2 (over x_hi).
Axes of the slice: x: 4 (x_hi: 2, x_lo: 2; x = x_hi * 2 + x_lo), y: 8, z: 8, core: 2. Of those that a mesh axis runs over, the one named last changes fastest.
Arguments:
- queries: bfloat16 [384, 32, 8, 2048], P(('rep', 'tm'), 'height'), parts along dimension 0, may hold values from -6 to 6
- key_tokens: bfloat16 [384, 32, 8, 2048], P(('rep', 'tm'), 'height'), parts along dimension 0, may hold values from -6 to 6
- value_tokens: bfloat16 [384, 32, 8, 2048], P(('rep', 'tm'), 'height'), parts along dimension 0, may hold values from -6 to 6
- text_keys: bfloat16 [512, 2048], P(('rep', 'tm'), 'height'), parts along dimension 0, may hold values from -8 to 8
- text_values: bfloat16 [512, 2048], P(('rep', 'tm'), 'height'), parts along dimension 0, may hold values from -6 to 6
- text_length: int32 [2], P('rep'), parts along dimension 0, may hold values from 32 to 256
Outputs:
- attended: bfloat16 [384, 32, 8, 2048], P(('rep', 'tm'), 'height'), parts along dimension 0
The draws below stay inside these ranges and needn't reach their ends.
There are 2 independent parts, one for each index of `rep`. The reference program is written for one: setup_inputs(seed, part) draws one part's arguments, and reference() takes and returns one part's arrays. A program takes and returns all parts, laid end to end along the dimension named above; each array names one. Nothing has to cross between parts.
All inputs are finite; a program needn't handle non-finite values.
Results may differ from the reference program's by a relative error of at most 0.005.
Values may be sent and summed in bfloat16 or wider, within the bound.
A program may use at most 64 MiB of HBM per device.

```python
import jax
import jax.numpy as jnp
from jax import lax

H = 16
DH = 128
TF = 6
TH = 8
NW = 8
TXT = 256
NF = 192
NH = 32


def draw_queries(key, part):
    key = jax.random.fold_in(key, 5)
    result = jnp.clip(jax.random.normal(key, (NF, NH, NW, H * DH)), -6.0, 6.0)
    return result.astype(jnp.bfloat16)


def draw_key_tokens(key, part):
    key = jax.random.fold_in(key, 9)
    result = jnp.clip(jax.random.normal(key, (NF, NH, NW, H * DH)), -6.0, 6.0)
    return result.astype(jnp.bfloat16)


def levels(rng, dims, cuts, low, largest):
    factor_of = 1.0
    for dim, shards_of in cuts:
        draws = jax.random.uniform(jax.random.fold_in(jax.random.fold_in(rng, 6), dim), (shards_of,), jnp.float32, low / len(cuts), largest / len(cuts))
        factor_of = factor_of * jnp.repeat(jnp.exp(draws), dims[dim] // shards_of).reshape((-1,) + (1,) * (len(dims) - 1 - dim))
    return factor_of


def bell_draw(stream_key, shape, spread, reach, cuts=(), kind=jnp.bfloat16):
    values = spread * jax.random.normal(stream_key, shape, jnp.float32)
    if cuts:
        values = values * levels(stream_key, shape, cuts, -0.22, 0.18)
    return jnp.clip(values, -reach, reach).astype(kind)


def setup_inputs(seed: int = 0, part: int = 0) -> dict:
    key_list = jax.random.split(jax.random.key(seed), 7)
    own_keys = jax.random.split(jax.random.fold_in(key_list[6], part), 7)
    queries = draw_queries(jax.random.fold_in(jax.random.fold_in(key_list[6], part), 71), part)
    key_tokens = draw_key_tokens(jax.random.fold_in(jax.random.fold_in(key_list[6], part), 71), part)
    value_tokens = bell_draw(own_keys[2], (NF, NH, NW, H * DH), 1.0, 6.0, ((0, 32), (1, 8)))
    text_keys = bell_draw(own_keys[3], (TXT, H * DH), 2.0, 8.0, ((0, 32), (1, 8)))
    text_values = bell_draw(own_keys[4], (TXT, H * DH), 1.0, 6.0, ((0, 32), (1, 8)))
    text_length = jax.random.randint(own_keys[5], (1,), TXT // 8, TXT + 1).astype(jnp.int32)
    return {"queries": queries, "key_tokens": key_tokens, "value_tokens": value_tokens, "text_keys": text_keys, "text_values": text_values, "text_length": text_length}


def reference(queries, key_tokens, value_tokens, text_keys, text_values, text_length):
    score_scale = 1.0 / (DH ** 0.5)
    time_tiles = NF // TF
    height_tiles = NH // TH
    feature_count = H * DH
    padding = ((2 * TF, 2 * TF), (2 * TH, 2 * TH), (0, 0), (0, 0))
    keys_padded = jnp.pad(key_tokens, padding)
    values_padded = jnp.pad(value_tokens, padding)
    text_key32 = text_keys.reshape(TXT, H, DH).astype(jnp.float32)
    text_value32 = text_values.reshape(TXT, H, DH).astype(jnp.float32)
    text_valid = jnp.arange(TXT, dtype=jnp.int32) < text_length[0]
    window_tiles = jnp.arange(3, dtype=jnp.int32)

    def one_tile(tile_number):
        time_tile = tile_number // height_tiles
        height_tile = tile_number % height_tiles
        anchor = jnp.zeros((), jnp.int32)
        query_block = lax.dynamic_slice(queries, (time_tile * TF, height_tile * TH, anchor, anchor), (TF, TH, NW, feature_count))
        starts = ((time_tile + 1) * TF, (height_tile + 1) * TH, anchor, anchor)
        key_block = lax.dynamic_slice(keys_padded, starts, (3 * TF, 3 * TH, NW, feature_count))
        value_block = lax.dynamic_slice(values_padded, starts, (3 * TF, 3 * TH, NW, feature_count))
        time_index = time_tile - 1 + window_tiles
        height_index = height_tile - 1 + window_tiles
        time_ok = jnp.repeat((time_index >= 0) & (time_index < time_tiles), TF)
        height_ok = jnp.repeat((height_index >= 0) & (height_index < height_tiles), TH)
        valid_keys = (time_ok[:, None, None] & height_ok[None, :, None] & jnp.ones((1, 1, NW), bool)).reshape(-1)
        query32 = query_block.reshape(-1, H, DH).astype(jnp.float32)
        key32 = key_block.reshape(-1, H, DH).astype(jnp.float32)
        value32 = value_block.reshape(-1, H, DH).astype(jnp.float32)
        window_scores = jnp.einsum("qhd,khd->hqk", query32, key32) * score_scale
        window_scores = jnp.where(valid_keys[None, None, :], window_scores, -jnp.inf)
        text_scores = jnp.einsum("qhd,khd->hqk", query32, text_key32) * score_scale
        text_scores = jnp.where(text_valid[None, None, :], text_scores, -jnp.inf)
        row_max = jnp.maximum(jnp.max(window_scores, -1), jnp.max(text_scores, -1))[:, :, None]
        window_weights = jnp.exp(window_scores - row_max)
        text_weights = jnp.exp(text_scores - row_max)
        denominator = jnp.sum(window_weights, -1) + jnp.sum(text_weights, -1)
        rounded = lax.optimization_barrier(window_weights.astype(jnp.bfloat16)).astype(jnp.float32)
        numerator = jnp.einsum("hqk,khd->hqd", rounded, value32) + jnp.einsum("hqk,khd->hqd", text_weights, text_value32)
        result = numerator / denominator[:, :, None]
        return jnp.transpose(result, (1, 0, 2)).reshape(TF, TH, NW, feature_count).astype(jnp.bfloat16)

    tile_results = lax.map(one_tile, jnp.arange(time_tiles * height_tiles, dtype=jnp.int32))
    tile_results = tile_results.reshape(time_tiles, height_tiles, TF, TH, NW, feature_count)
    return jnp.transpose(tile_results, (0, 2, 1, 3, 4, 5)).reshape(NF, NH, NW, feature_count)
```

```python
import functools
import math

import jax
import jax.numpy as jnp
from jax import lax
from jax.experimental import pallas as pl
from jax.experimental.pallas import tpu as pltpu
from jax.sharding import PartitionSpec as P

DH = 128
ZT = 2
LOG2E = 1.4426950408889634


def kernel(
    peers,
    frames_axis,
    heads,
    cells,
    text_rows,
    q_ref,
    k_ref,
    v_ref,
    tk_ref,
    tv_ref,
    len_ref,
    out_ref,
    kv,
    qh,
    oh,
    text,
    text_k,
    text_v,
    a2a_send,
    a2a_recv,
    halo_send,
    halo_recv,
    out_send,
    out_recv,
    text_send,
    text_recv,
    local_sem,
):
    me_t = lax.axis_index("tm")
    me_z = lax.axis_index("height")
    tiles = peers // ZT
    nxt = lax.rem(me_t + 1, frames_axis)
    prv = lax.rem(me_t + frames_axis - 1, frames_axis)

    def offset(j):
        return jnp.where(lax.rem(j, 2) == 1, (j + 1) // 2, peers - j // 2)

    def columns(z, h):
        return pl.ds(pl.multiple_of((z * heads + h) * DH, DH), DH)

    barrier = pltpu.get_barrier_semaphore()

    def greet_z(j, c):
        pl.semaphore_signal(barrier, inc=1, device_id={"height": lax.rem(me_z + j, peers)})
        return c

    def greet_t(j, c):
        pl.semaphore_signal(barrier, inc=1, device_id={"tm": lax.rem(me_t + j, frames_axis)})
        return c

    lax.fori_loop(1, peers, greet_z, 0)
    lax.fori_loop(1, frames_axis, greet_t, 0)
    pl.semaphore_wait(barrier, peers - 1 + frames_axis - 1)

    sources = (k_ref, v_ref, q_ref)

    def landing(which, h, z):
        return qh.at[h, z] if which == 2 else kv.at[1, h, z, which]

    def a2a(which, h, d, z):
        return pltpu.make_async_remote_copy(
            src_ref=sources[which].at[:, columns(z, h)],
            dst_ref=landing(which, h, me_z),
            send_sem=a2a_send.at[h, which, d],
            recv_sem=a2a_recv.at[h, which, d],
            device_id={"height": z},
        )

    def arrival(which, h, d, z):
        return pltpu.make_async_remote_copy(
            src_ref=sources[which].at[:, columns(z, h)],
            dst_ref=landing(which, h, z),
            send_sem=a2a_send.at[h, which, d],
            recv_sem=a2a_recv.at[h, which, d],
            device_id={"height": z},
        )

    def own(which, h):
        return pltpu.make_async_copy(
            sources[which].at[:, columns(me_z, h)], landing(which, h, me_z), local_sem.at[h, which]
        )

    def send_all(which_list, h):
        def step(j, c):
            d = offset(j)
            z = lax.rem(me_z + d, peers)
            for which in which_list:
                a2a(which, h, d, z).start()
            return c

        lax.fori_loop(1, peers, step, 0)

    def halo(h, z, side):
        return pltpu.make_async_remote_copy(
            src_ref=kv.at[1, h, z],
            dst_ref=kv.at[2 * side, h, z],
            send_sem=halo_send.at[h, side, z],
            recv_sem=halo_recv.at[h, side, z],
            device_id={"tm": nxt if side == 0 else prv},
        )

    def forward(h):
        for which in range(2):
            own(which, h).wait()
        for side in range(2):
            halo(h, me_z, side).start()

        def step(j, c):
            d = offset(j)
            z = lax.rem(me_z + peers - d, peers)
            for which in range(2):
                arrival(which, h, d, z).wait_recv()
            for side in range(2):
                halo(h, z, side).start()
            return c

        lax.fori_loop(1, peers, step, 0)

    for h in range(heads):
        for which in range(3):
            own(which, h).start()
    send_all((0, 1), 0)

    text[me_t, :, : heads * DH] = tk_ref[...].astype(jnp.float32)
    text[me_t, :, heads * DH :] = tv_ref[...].astype(jnp.float32)

    def text_step(j, c):
        pltpu.make_async_remote_copy(
            src_ref=text.at[me_t],
            dst_ref=text.at[me_t],
            send_sem=text_send,
            recv_sem=text_recv,
            device_id={"tm": lax.rem(me_t + j, frames_axis)},
        ).start()
        return c

    lax.fori_loop(1, frames_axis, text_step, 0)
    for h in range(1, heads):
        send_all((0, 1), h)
    forward(0)
    for h in range(heads):
        send_all((2,), h)
    for h in range(1, heads):
        forward(h)

    rest = text.at[pl.ds(1, frames_axis - 1)]
    all_text = pltpu.make_async_remote_copy(
        src_ref=rest, dst_ref=rest, send_sem=text_send, recv_sem=text_recv, device_id={"tm": nxt}
    )
    all_text.wait()
    for h in range(heads):
        lane = slice(h * DH, (h + 1) * DH)
        lane_v = slice((heads + h) * DH, (heads + h + 1) * DH)
        text_k[h] = text[:, :, lane].reshape(-1, DH).astype(jnp.bfloat16)
        text_v[h] = text[:, :, lane_v].reshape(-1, DH).astype(jnp.bfloat16)

    scale = LOG2E / math.sqrt(DH)
    first = jnp.where(me_t == 0, 1, 0)
    last = jnp.where(me_t == frames_axis - 1, 2, 3)

    def scores_of(q, k):
        s = lax.dot_general(q, k, (((1,), (1,)), ((), ())), preferred_element_type=jnp.float32)
        return s * scale

    def tile(h, a, start, count):
        rows = ZT * cells
        q = qh[h, pl.ds(ZT * a, ZT)].reshape(rows, DH)
        s = scores_of(q, text_k[h])
        place = lax.broadcasted_iota(jnp.int32, s.shape, 1)
        s = jnp.where(place < len_ref[0], s, -jnp.inf)
        top = jnp.max(s, 1, keepdims=True)
        p = jnp.exp2(s - top)
        total = jnp.sum(p, 1, keepdims=True)
        acc = jnp.dot(p.astype(jnp.bfloat16), text_v[h], preferred_element_type=jnp.float32)

        def window(t, carry):
            top, total, acc = carry
            k = kv[t, h, pl.ds(start, count), 0].reshape(count * cells, DH)
            v = kv[t, h, pl.ds(start, count), 1].reshape(count * cells, DH)
            s = scores_of(q, k)
            new = jnp.maximum(top, jnp.max(s, 1, keepdims=True))
            fade = jnp.exp2(top - new)
            p = jnp.exp2(s - new)
            total = total * fade + jnp.sum(p, 1, keepdims=True)
            acc = acc * fade + jnp.dot(
                p.astype(jnp.bfloat16), v, preferred_element_type=jnp.float32
            )
            return new, total, acc

        top, total, acc = lax.fori_loop(first, last, window, (top, total, acc))
        oh[h, pl.ds(ZT * a, ZT)] = (
            (acc / total).astype(jnp.bfloat16).reshape(ZT, cells, DH)
        )

    def result(h, z):
        return pltpu.make_async_remote_copy(
            src_ref=oh.at[h, z],
            dst_ref=out_ref.at[:, columns(me_z, h)],
            send_sem=out_send.at[h, z],
            recv_sem=out_recv.at[h, me_z],
            device_id={"height": z},
        )

    def result_own(h):
        return pltpu.make_async_copy(
            oh.at[h, me_z], out_ref.at[:, columns(me_z, h)], out_send.at[h, me_z]
        )

    def send_tile(h, a):
        for i in range(ZT):
            z = ZT * a + i

            @pl.when(z != me_z)
            def _():
                result(h, z).start()

            @pl.when(z == me_z)
            def _():
                result_own(h).start()

    for h in range(heads):
        own(2, h).wait()

        def q_step(j, c, h=h):
            d = offset(j)
            arrival(2, h, d, lax.rem(me_z + peers - d, peers)).wait_recv()
            return c

        lax.fori_loop(1, peers, q_step, 0)

        def halo_step(z, c, h=h):
            for side in range(2):
                halo(h, z, side).wait_recv()
            return c

        lax.fori_loop(0, peers, halo_step, 0)

        def edge(i, c, h=h):
            a = i * (tiles - 1)
            tile(h, a, a * ZT - i * ZT, 2 * ZT)
            send_tile(h, a)
            return c

        def inner(a, c, h=h):
            tile(h, a, (a - 1) * ZT, 3 * ZT)
            send_tile(h, a)
            return c

        lax.fori_loop(0, 2, edge, 0)
        lax.fori_loop(1, tiles - 1, inner, 0)

    for h in range(heads):
        result_own(h).wait()

        def end_step(j, c, h=h):
            d = offset(j)
            z = lax.rem(me_z + d, peers)
            for which in range(3):
                a2a(which, h, d, z).wait_send()
            result(h, z).wait_send()
            pltpu.make_async_remote_copy(
                src_ref=oh.at[h, z],
                dst_ref=out_ref.at[:, columns(z, h)],
                send_sem=out_send.at[h, z],
                recv_sem=out_recv.at[h, z],
                device_id={"height": z},
            ).wait_recv()
            return c

        lax.fori_loop(1, peers, end_step, 0)

        def halo_end(z, c, h=h):
            for side in range(2):
                halo(h, z, side).wait_send()
            return c

        lax.fori_loop(0, peers, halo_end, 0)


def per_device(queries, key_tokens, value_tokens, text_keys, text_values, text_length):
    shape = queries.shape
    features = shape[3]
    cells = shape[0] * shape[1] * shape[2]
    peers = lax.axis_size("height")
    frames_axis = lax.axis_size("tm")
    heads = features // DH // peers
    text_rows = text_keys.shape[0]
    flat = [x.reshape(cells, features) for x in (queries, key_tokens, value_tokens)]
    any_space = pl.BlockSpec(memory_space=pl.ANY)
    vmem = pl.BlockSpec(memory_space=pltpu.VMEM)
    dma = pltpu.SemaphoreType.DMA
    result = pl.pallas_call(
        functools.partial(kernel, peers, frames_axis, heads, cells, text_rows),
        out_shape=jax.ShapeDtypeStruct((cells, features), jnp.bfloat16),
        in_specs=[any_space] * 3 + [vmem] * 2 + [pl.BlockSpec(memory_space=pltpu.SMEM)],
        out_specs=any_space,
        scratch_shapes=[
            pltpu.VMEM((3, heads, peers, 2, cells, DH), jnp.bfloat16),
            pltpu.VMEM((heads, peers, cells, DH), jnp.bfloat16),
            pltpu.VMEM((heads, peers, cells, DH), jnp.bfloat16),
            pltpu.VMEM((frames_axis, text_rows, 2 * heads * DH), jnp.float32),
            pltpu.VMEM((heads, frames_axis * text_rows, DH), jnp.bfloat16),
            pltpu.VMEM((heads, frames_axis * text_rows, DH), jnp.bfloat16),
            dma((heads, 3, peers)),
            dma((heads, 3, peers)),
            dma((heads, 2, peers)),
            dma((heads, 2, peers)),
            dma((heads, peers)),
            dma((heads, peers)),
            dma,
            dma,
            dma((heads, 3)),
        ],
        compiler_params=pltpu.CompilerParams(
            collective_id=0, has_side_effects=True, vmem_limit_bytes=62 * 1024 * 1024
        ),
        cost_estimate=pl.CostEstimate(
            flops=5_000_000_000, bytes_accessed=4_000_000, transcendentals=10_000_000
        ),
    )(*flat, text_keys, text_values, text_length)
    return result.reshape(shape)


def solution(mesh):
    placed = (
        P(("rep", "tm"), "height", None, None),
        P(("rep", "tm"), "height", None, None),
        P(("rep", "tm"), "height", None, None),
        P(("rep", "tm"), "height"),
        P(("rep", "tm"), "height"),
        P("rep"),
    )
    return jax.shard_map(
        per_device,
        mesh=mesh,
        in_specs=placed,
        out_specs=P(("rep", "tm"), "height", None, None),
        check_vma=False,
    )
```

```python
import functools
import math

import jax
import jax.numpy as jnp
from jax import lax
from jax.experimental import pallas as pl
from jax.experimental.pallas import tpu as pltpu
from jax.sharding import PartitionSpec as P

DH = 128
ZT = 2
LOG2E = 1.4426950408889634


def kernel(
    peers,
    frames_axis,
    heads,
    cells,
    text_rows,
    q_ref,
    k_ref,
    v_ref,
    tk_ref,
    tv_ref,
    len_ref,
    out_ref,
    kv,
    qh,
    oh,
    text,
    text_k,
    text_v,
    text_s,
    scores,
    weights,
    a2a_send,
    a2a_recv,
    halo_send,
    halo_recv,
    out_send,
    out_recv,
    text_send,
    text_recv,
    local_sem,
):
    me_t = lax.axis_index("tm")
    me_z = lax.axis_index("height")
    tiles = peers // ZT
    nxt = lax.rem(me_t + 1, frames_axis)
    prv = lax.rem(me_t + frames_axis - 1, frames_axis)

    def offset(j):
        return jnp.where(lax.rem(j, 2) == 1, (j + 1) // 2, peers - j // 2)

    def columns(z, h):
        return pl.ds(pl.multiple_of((z * heads + h) * DH, DH), DH)

    barrier = pltpu.get_barrier_semaphore()

    def greet_z(j, c):
        pl.semaphore_signal(barrier, inc=1, device_id={"height": lax.rem(me_z + j, peers)})
        return c

    def greet_t(j, c):
        pl.semaphore_signal(barrier, inc=1, device_id={"tm": lax.rem(me_t + j, frames_axis)})
        return c

    lax.fori_loop(1, peers, greet_z, 0)
    lax.fori_loop(1, frames_axis, greet_t, 0)
    pl.semaphore_wait(barrier, peers - 1 + frames_axis - 1)

    sources = (k_ref, v_ref, q_ref)

    def landing(which, h, z):
        return qh.at[h, z] if which == 2 else kv.at[1, h, z, which]

    def a2a(which, h, d, z):
        return pltpu.make_async_remote_copy(
            src_ref=sources[which].at[:, columns(z, h)],
            dst_ref=landing(which, h, me_z),
            send_sem=a2a_send.at[h, which, d],
            recv_sem=a2a_recv.at[h, which, d],
            device_id={"height": z},
        )

    def arrival(which, h, d, z):
        return pltpu.make_async_remote_copy(
            src_ref=sources[which].at[:, columns(z, h)],
            dst_ref=landing(which, h, z),
            send_sem=a2a_send.at[h, which, d],
            recv_sem=a2a_recv.at[h, which, d],
            device_id={"height": z},
        )

    def own(which, h):
        return pltpu.make_async_copy(
            sources[which].at[:, columns(me_z, h)], landing(which, h, me_z), local_sem.at[h, which]
        )

    def send_all(which_list, h):
        def step(j, c):
            d = offset(j)
            z = lax.rem(me_z + d, peers)
            for which in which_list:
                a2a(which, h, d, z).start()
            return c

        lax.fori_loop(1, peers, step, 0)

    def halo(h, z, side):
        return pltpu.make_async_remote_copy(
            src_ref=kv.at[1, h, z],
            dst_ref=kv.at[2 * side, h, z],
            send_sem=halo_send.at[h, side, z],
            recv_sem=halo_recv.at[h, side, z],
            device_id={"tm": nxt if side == 0 else prv},
        )

    def forward(h):
        for which in range(2):
            own(which, h).wait()
        for side in range(2):
            halo(h, me_z, side).start()

        def step(j, c):
            d = offset(j)
            z = lax.rem(me_z + peers - d, peers)
            for which in range(2):
                arrival(which, h, d, z).wait_recv()
            for side in range(2):
                halo(h, z, side).start()
            return c

        lax.fori_loop(1, peers, step, 0)

    for h in range(heads):
        for which in range(3):
            own(which, h).start()
    send_all((0, 1), 0)

    text[me_t, :, : heads * DH] = tk_ref[...].astype(jnp.float32)
    text[me_t, :, heads * DH :] = tv_ref[...].astype(jnp.float32)

    def text_step(j, c):
        pltpu.make_async_remote_copy(
            src_ref=text.at[me_t],
            dst_ref=text.at[me_t],
            send_sem=text_send,
            recv_sem=text_recv,
            device_id={"tm": lax.rem(me_t + j, frames_axis)},
        ).start()
        return c

    lax.fori_loop(1, frames_axis, text_step, 0)
    send_all((2,), 0)
    forward(0)

    for h in range(1, heads):
        send_all((0, 1), h)
    rest = text.at[pl.ds(1, frames_axis - 1)]
    all_text = pltpu.make_async_remote_copy(
        src_ref=rest, dst_ref=rest, send_sem=text_send, recv_sem=text_recv, device_id={"tm": nxt}
    )
    all_text.wait()
    for h in range(heads):
        lane = slice(h * DH, (h + 1) * DH)
        lane_v = slice((heads + h) * DH, (heads + h + 1) * DH)
        text_k[h] = text[:, :, lane].reshape(-1, DH).astype(jnp.bfloat16)
        text_v[h] = text[:, :, lane_v].reshape(-1, DH).astype(jnp.bfloat16)

    scale = LOG2E / math.sqrt(DH)
    rows = ZT * cells
    bias = (
        jnp.where(me_t == 0, -jnp.inf, 0.0).astype(jnp.float32),
        jnp.float32(0.0),
        jnp.where(me_t == frames_axis - 1, -jnp.inf, 0.0).astype(jnp.float32),
    )
    ones = jnp.ones((3 * ZT * cells, DH), jnp.bfloat16)

    def product(q, k):
        return lax.dot_general(q, k, (((1,), (1,)), ((), ())), preferred_element_type=jnp.float32)

    def lanes_max(s):
        parts = [s[:, i : i + DH] for i in range(0, s.shape[1], DH)]
        return functools.reduce(jnp.maximum, parts)

    def weights_of(s, shift):
        parts = [
            jnp.exp2(s[:, i : i + DH] * scale - shift).astype(jnp.bfloat16)
            for i in range(0, s.shape[1], DH)
        ]
        return jnp.concatenate(parts, 1)

    def tile(h, a, start, count):
        n = count * cells
        chunks = [(c, min(256, n - c)) for c in range(0, n, 256)]
        q = qh[h, pl.ds(ZT * a, ZT)].reshape(rows, DH)
        s = product(q, text_k[h])
        place = lax.broadcasted_iota(jnp.int32, s.shape, 1)
        s = jnp.where(place < len_ref[0], s, -jnp.inf)
        text_s[...] = s
        top = lanes_max(s)
        for t in range(3):
            k = kv[t, h, pl.ds(start, count), 0].reshape(n, DH)
            part = None
            for c, w in chunks:
                s = product(q, k[c : c + w])
                scores[t, :, c : c + w] = s
                m = lanes_max(s)
                part = m if part is None else jnp.maximum(part, m)
            top = jnp.maximum(top, part + bias[t])
        top = jnp.broadcast_to(jnp.max(top, 1, keepdims=True) * scale, (rows, DH))

        acc = jnp.dot(
            weights_of(text_s[...], top),
            jnp.concatenate([text_v[h], ones[: text_v.shape[1]]], 1),
            preferred_element_type=jnp.float32,
        )
        for t in range(3):
            shift = top - bias[t]
            for c, w in chunks:
                weights[t, :, c : c + w] = weights_of(scores[t, :, c : c + w], shift)
            v = kv[t, h, pl.ds(start, count), 1].reshape(n, DH)
            acc = acc + jnp.dot(
                weights[t, :, :n],
                jnp.concatenate([v, ones[:n]], 1),
                preferred_element_type=jnp.float32,
            )
        oh[h, pl.ds(ZT * a, ZT)] = (
            (acc[:, :DH] / acc[:, DH:]).astype(jnp.bfloat16).reshape(ZT, cells, DH)
        )

    def result(h, z):
        return pltpu.make_async_remote_copy(
            src_ref=oh.at[h, z],
            dst_ref=out_ref.at[:, columns(me_z, h)],
            send_sem=out_send.at[h, z],
            recv_sem=out_recv.at[h, me_z],
            device_id={"height": z},
        )

    def result_own(h):
        return pltpu.make_async_copy(
            oh.at[h, me_z], out_ref.at[:, columns(me_z, h)], out_send.at[h, me_z]
        )

    def send_tile(h, a):
        for i in range(ZT):
            z = ZT * a + i

            @pl.when(z != me_z)
            def _():
                result(h, z).start()

            @pl.when(z == me_z)
            def _():
                result_own(h).start()

    def wait_queries(h):
        def q_step(j, c):
            d = offset(j)
            arrival(2, h, d, lax.rem(me_z + peers - d, peers)).wait_recv()
            return c

        own(2, h).wait()
        lax.fori_loop(1, peers, q_step, 0)

    for h in range(heads):
        if h > 0:
            forward(h)
        wait_queries(h)
        if h + 1 < heads:
            send_all((2,), h + 1)

        def halo_step(z, c, h=h):
            for side in range(2):
                halo(h, z, side).wait_recv()
            return c

        lax.fori_loop(0, peers, halo_step, 0)

        def tile_step(i, c, h=h):
            side = 1 + 2 * lax.rem(me_t, 2)
            ahead = jnp.where(i == 0, 2, jnp.where(i == 1, side, jnp.where(i == 2, 4 - side, 0)))
            a = lax.rem(me_z // ZT + ahead, tiles)
            low = a == 0
            at_edge = jnp.logical_or(low, a == tiles - 1)

            @pl.when(at_edge)
            def _():
                tile(h, a, jnp.where(low, 0, (tiles - 2) * ZT), 2 * ZT)

            @pl.when(jnp.logical_not(at_edge))
            def _():
                tile(h, a, (a - 1) * ZT, 3 * ZT)

            send_tile(h, a)
            return c

        lax.fori_loop(0, tiles, tile_step, 0)

    for h in range(heads):
        result_own(h).wait()

        def end_step(j, c, h=h):
            d = offset(j)
            z = lax.rem(me_z + d, peers)
            for which in range(3):
                a2a(which, h, d, z).wait_send()
            result(h, z).wait_send()
            pltpu.make_async_remote_copy(
                src_ref=oh.at[h, z],
                dst_ref=out_ref.at[:, columns(z, h)],
                send_sem=out_send.at[h, z],
                recv_sem=out_recv.at[h, z],
                device_id={"height": z},
            ).wait_recv()
            return c

        lax.fori_loop(1, peers, end_step, 0)

        def halo_end(z, c, h=h):
            for side in range(2):
                halo(h, z, side).wait_send()
            return c

        lax.fori_loop(0, peers, halo_end, 0)


def per_device(queries, key_tokens, value_tokens, text_keys, text_values, text_length):
    shape = queries.shape
    features = shape[3]
    cells = shape[0] * shape[1] * shape[2]
    peers = lax.axis_size("height")
    frames_axis = lax.axis_size("tm")
    heads = features // DH // peers
    text_rows = text_keys.shape[0]
    flat = [x.reshape(cells, features) for x in (queries, key_tokens, value_tokens)]
    any_space = pl.BlockSpec(memory_space=pl.ANY)
    vmem = pl.BlockSpec(memory_space=pltpu.VMEM)
    dma = pltpu.SemaphoreType.DMA
    result = pl.pallas_call(
        functools.partial(kernel, peers, frames_axis, heads, cells, text_rows),
        out_shape=jax.ShapeDtypeStruct((cells, features), jnp.bfloat16),
        in_specs=[any_space] * 3 + [vmem] * 2 + [pl.BlockSpec(memory_space=pltpu.SMEM)],
        out_specs=any_space,
        scratch_shapes=[
            pltpu.VMEM((3, heads, peers, 2, cells, DH), jnp.bfloat16),
            pltpu.VMEM((heads, peers, cells, DH), jnp.bfloat16),
            pltpu.VMEM((heads, peers, cells, DH), jnp.bfloat16),
            pltpu.VMEM((frames_axis, text_rows, 2 * heads * DH), jnp.float32),
            pltpu.VMEM((heads, frames_axis * text_rows, DH), jnp.bfloat16),
            pltpu.VMEM((heads, frames_axis * text_rows, DH), jnp.bfloat16),
            pltpu.VMEM((ZT * cells, frames_axis * text_rows), jnp.float32),
            pltpu.VMEM((3, ZT * cells, 3 * ZT * cells), jnp.float32),
            pltpu.VMEM((3, ZT * cells, 3 * ZT * cells), jnp.bfloat16),
            dma((heads, 3, peers)),
            dma((heads, 3, peers)),
            dma((heads, 2, peers)),
            dma((heads, 2, peers)),
            dma((heads, peers)),
            dma((heads, peers)),
            dma,
            dma,
            dma((heads, 3)),
        ],
        compiler_params=pltpu.CompilerParams(
            collective_id=0, has_side_effects=True, vmem_limit_bytes=62 * 1024 * 1024
        ),
        cost_estimate=pl.CostEstimate(
            flops=5_000_000_000, bytes_accessed=4_000_000, transcendentals=10_000_000
        ),
    )(*flat, text_keys, text_values, text_length)
    return result.reshape(shape)


def solution(mesh):
    placed = (
        P(("rep", "tm"), "height", None, None),
        P(("rep", "tm"), "height", None, None),
        P(("rep", "tm"), "height", None, None),
        P(("rep", "tm"), "height"),
        P(("rep", "tm"), "height"),
        P("rep"),
    )
    return jax.shard_map(
        per_device,
        mesh=mesh,
        in_specs=placed,
        out_specs=P(("rep", "tm"), "height", None, None),
        check_vma=False,
    )
```

```python
import functools
import math

import jax
import jax.numpy as jnp
from jax import lax
from jax.experimental import pallas as pl
from jax.experimental.pallas import tpu as pltpu
from jax.sharding import PartitionSpec as P

DH = 128
ZT = 2
LOG2E = 1.4426950408889634


def kernel(
    peers,
    frames_axis,
    heads,
    cells,
    text_rows,
    q_ref,
    k_ref,
    v_ref,
    tk_ref,
    tv_ref,
    len_ref,
    out_ref,
    kv,
    qh,
    oh,
    relay,
    text,
    text_k,
    text_v,
    text_s,
    scores,
    weights,
    a2a_send,
    a2a_recv,
    halo_send,
    halo_recv,
    out_send,
    out_recv,
    hop_send,
    hop_recv,
    pass_send,
    text_send,
    text_recv,
    local_sem,
):
    me_t = lax.axis_index("tm")
    me_z = lax.axis_index("height")
    tiles = peers // ZT
    nxt = lax.rem(me_t + 1, frames_axis)
    prv = lax.rem(me_t + frames_axis - 1, frames_axis)

    def offset(j):
        return jnp.where(lax.rem(j, 2) == 1, (j + 1) // 2, peers - j // 2)

    def columns(z, h):
        return pl.ds(pl.multiple_of((z * heads + h) * DH, DH), DH)

    barrier = pltpu.get_barrier_semaphore()

    def greet_z(j, c):
        pl.semaphore_signal(barrier, inc=1, device_id={"height": lax.rem(me_z + j, peers)})
        return c

    def greet_t(j, c):
        pl.semaphore_signal(barrier, inc=1, device_id={"tm": lax.rem(me_t + j, frames_axis)})
        return c

    lax.fori_loop(1, peers, greet_z, 0)
    lax.fori_loop(1, frames_axis, greet_t, 0)
    pl.semaphore_wait(barrier, peers - 1 + frames_axis - 1)

    sources = (k_ref, v_ref, q_ref)

    def landing(which, h, z):
        return qh.at[h, z] if which == 2 else kv.at[1, h, z, which]

    def a2a(which, h, d, z):
        return pltpu.make_async_remote_copy(
            src_ref=sources[which].at[:, columns(z, h)],
            dst_ref=landing(which, h, me_z),
            send_sem=a2a_send.at[h, which, d],
            recv_sem=a2a_recv.at[h, which, d],
            device_id={"height": z},
        )

    def arrival(which, h, d, z):
        return pltpu.make_async_remote_copy(
            src_ref=sources[which].at[:, columns(z, h)],
            dst_ref=landing(which, h, z),
            send_sem=a2a_send.at[h, which, d],
            recv_sem=a2a_recv.at[h, which, d],
            device_id={"height": z},
        )

    def own(which, h):
        return pltpu.make_async_copy(
            sources[which].at[:, columns(me_z, h)], landing(which, h, me_z), local_sem.at[h, which]
        )

    opposite = lax.rem(me_z + peers // 2, peers)

    def half(side):
        return pl.ds(side * (cells // 2), cells // 2)

    def shifted(by):
        return lax.rem(me_z + peers + by, peers)

    def hop(which, h, side):
        if which == 3:
            source = oh.at[h, opposite, half(side)]
        else:
            source = sources[which].at[half(side), columns(opposite, h)]
        return pltpu.make_async_remote_copy(
            src_ref=source,
            dst_ref=relay.at[h, which, side],
            send_sem=hop_send.at[h, which, side],
            recv_sem=hop_recv.at[h, which, side],
            device_id={"height": shifted(1 - 2 * side)},
        )

    def pass_on(which, h, side):
        origin = shifted(2 * side - 1)
        if which == 3:
            target, counted = out_ref.at[half(side), columns(origin, h)], out_recv.at[h, origin]
        else:
            counted = a2a_recv.at[h, which, peers // 2]
            if which == 2:
                target = qh.at[h, origin, half(side)]
            else:
                target = kv.at[1, h, origin, which, half(side)]
        return pltpu.make_async_remote_copy(
            src_ref=relay.at[h, which, side],
            dst_ref=target,
            send_sem=pass_send.at[h, which, side],
            recv_sem=counted,
            device_id={"height": shifted((1 - 2 * side) * (peers // 2 - 1))},
        )

    def relay_step(which, h):
        for side in range(2):
            hop(which, h, side).wait_recv()
            pass_on(which, h, side).start()

    def send_all(which_list, h, farthest_first=False):
        for which in which_list:
            for side in range(2):
                hop(which, h, side).start()

        def step(j, c):
            d = offset(peers - 1 - j if farthest_first else j)
            z = lax.rem(me_z + d, peers)
            for which in which_list:
                a2a(which, h, d, z).start()
            return c

        lax.fori_loop(1, peers - 1, step, 0)

    def halo(h, z, side):
        return pltpu.make_async_remote_copy(
            src_ref=kv.at[1, h, z],
            dst_ref=kv.at[2 * side, h, z],
            send_sem=halo_send.at[h, side, z],
            recv_sem=halo_recv.at[h, side, z],
            device_id={"tm": nxt if side == 0 else prv},
        )

    def forward(h):
        for which in range(2):
            own(which, h).wait()
        for side in range(2):
            halo(h, me_z, side).start()
        for which in range(2):
            relay_step(which, h)

        def step(j, c):
            d = offset(j)
            z = lax.rem(me_z + peers - d, peers)
            for which in range(2):
                arrival(which, h, d, z).wait_recv()
            for side in range(2):
                halo(h, z, side).start()
            return c

        lax.fori_loop(1, peers, step, 0)

    for h in range(heads):
        for which in range(3):
            own(which, h).start()
    send_all((0, 1), 0)

    text[me_t, :, : heads * DH] = tk_ref[...].astype(jnp.float32)
    text[me_t, :, heads * DH :] = tv_ref[...].astype(jnp.float32)

    def text_step(j, c):
        pltpu.make_async_remote_copy(
            src_ref=text.at[me_t],
            dst_ref=text.at[me_t],
            send_sem=text_send,
            recv_sem=text_recv,
            device_id={"tm": lax.rem(me_t + j, frames_axis)},
        ).start()
        return c

    lax.fori_loop(1, frames_axis, text_step, 0)
    send_all((2,), 0, True)
    forward(0)

    for h in range(1, heads):
        send_all((0, 1), h)
    rest = text.at[pl.ds(1, frames_axis - 1)]
    all_text = pltpu.make_async_remote_copy(
        src_ref=rest, dst_ref=rest, send_sem=text_send, recv_sem=text_recv, device_id={"tm": nxt}
    )
    all_text.wait()
    for h in range(heads):
        lane = slice(h * DH, (h + 1) * DH)
        lane_v = slice((heads + h) * DH, (heads + h + 1) * DH)
        text_k[h] = text[:, :, lane].reshape(-1, DH).astype(jnp.bfloat16)
        text_v[h] = text[:, :, lane_v].reshape(-1, DH).astype(jnp.bfloat16)

    scale = LOG2E / math.sqrt(DH)
    rows = ZT * cells
    bias = (
        jnp.where(me_t == 0, -jnp.inf, 0.0).astype(jnp.float32),
        jnp.float32(0.0),
        jnp.where(me_t == frames_axis - 1, -jnp.inf, 0.0).astype(jnp.float32),
    )
    ones = jnp.ones((3 * ZT * cells, DH), jnp.bfloat16)

    def product(q, k):
        return lax.dot_general(q, k, (((1,), (1,)), ((), ())), preferred_element_type=jnp.float32)

    def lanes_max(s):
        parts = [s[:, i : i + DH] for i in range(0, s.shape[1], DH)]
        return functools.reduce(jnp.maximum, parts)

    def weights_of(s, shift):
        parts = [
            jnp.exp2(s[:, i : i + DH] * scale - shift).astype(jnp.bfloat16)
            for i in range(0, s.shape[1], DH)
        ]
        return jnp.concatenate(parts, 1)

    def tile(h, a, start, count):
        n = count * cells
        chunks = [(c, min(256, n - c)) for c in range(0, n, 256)]
        q = qh[h, pl.ds(ZT * a, ZT)].reshape(rows, DH)
        s = product(q, text_k[h])
        place = lax.broadcasted_iota(jnp.int32, s.shape, 1)
        s = jnp.where(place < len_ref[0], s, -jnp.inf)
        text_s[...] = s
        top = lanes_max(s)
        for t in range(3):
            k = kv[t, h, pl.ds(start, count), 0].reshape(n, DH)
            part = None
            for c, w in chunks:
                s = product(q, k[c : c + w])
                scores[t, :, c : c + w] = s
                m = lanes_max(s)
                part = m if part is None else jnp.maximum(part, m)
            top = jnp.maximum(top, part + bias[t])
        top = jnp.broadcast_to(jnp.max(top, 1, keepdims=True) * scale, (rows, DH))

        acc = jnp.dot(
            weights_of(text_s[...], top),
            jnp.concatenate([text_v[h], ones[: text_v.shape[1]]], 1),
            preferred_element_type=jnp.float32,
        )
        for t in range(3):
            shift = top - bias[t]
            for c, w in chunks:
                weights[t, :, c : c + w] = weights_of(scores[t, :, c : c + w], shift)
            v = kv[t, h, pl.ds(start, count), 1].reshape(n, DH)
            acc = acc + jnp.dot(
                weights[t, :, :n],
                jnp.concatenate([v, ones[:n]], 1),
                preferred_element_type=jnp.float32,
            )
        oh[h, pl.ds(ZT * a, ZT)] = (
            (acc[:, :DH] / acc[:, DH:]).astype(jnp.bfloat16).reshape(ZT, cells, DH)
        )

    def result(h, z):
        return pltpu.make_async_remote_copy(
            src_ref=oh.at[h, z],
            dst_ref=out_ref.at[:, columns(me_z, h)],
            send_sem=out_send.at[h, z],
            recv_sem=out_recv.at[h, me_z],
            device_id={"height": z},
        )

    def result_arrival(h, z):
        return pltpu.make_async_remote_copy(
            src_ref=oh.at[h, z],
            dst_ref=out_ref.at[:, columns(z, h)],
            send_sem=out_send.at[h, z],
            recv_sem=out_recv.at[h, z],
            device_id={"height": z},
        )

    def result_own(h):
        return pltpu.make_async_copy(
            oh.at[h, me_z], out_ref.at[:, columns(me_z, h)], out_send.at[h, me_z]
        )

    def send_tile(h, a):
        for i in range(ZT):
            z = ZT * a + i

            @pl.when(jnp.logical_and(z != me_z, z != opposite))
            def _():
                result(h, z).start()

            @pl.when(z == opposite)
            def _():
                for side in range(2):
                    hop(3, h, side).start()

            @pl.when(z == me_z)
            def _():
                result_own(h).start()

    def wait_queries(h, a):
        for i in range(ZT):
            z = ZT * a + i

            @pl.when(z != me_z)
            def _():
                arrival(2, h, lax.rem(me_z + peers - z, peers), z).wait_recv()

            @pl.when(z == me_z)
            def _():
                own(2, h).wait()

    for h in range(heads):
        if h > 0:
            forward(h)
        if h + 1 < heads:
            send_all((2,), h + 1, True)
        relay_step(2, h)

        def halo_step(z, c, h=h):
            for side in range(2):
                halo(h, z, side).wait_recv()
            return c

        lax.fori_loop(0, peers, halo_step, 0)

        def tile_step(i, c, h=h):
            side = 1 + 2 * lax.rem(me_t, 2)
            ahead = jnp.where(i == 0, 2, jnp.where(i == 1, side, jnp.where(i == 2, 4 - side, 0)))
            a = lax.rem(me_z // ZT + ahead, tiles)
            low = a == 0
            at_edge = jnp.logical_or(low, a == tiles - 1)
            wait_queries(h, a)

            @pl.when(i == 2)
            def _():
                relay_step(3, h)

            @pl.when(at_edge)
            def _():
                tile(h, a, jnp.where(low, 0, (tiles - 2) * ZT), 2 * ZT)

            @pl.when(jnp.logical_not(at_edge))
            def _():
                tile(h, a, (a - 1) * ZT, 3 * ZT)

            send_tile(h, a)
            return c

        lax.fori_loop(0, tiles, tile_step, 0)

    for h in range(heads):
        result_own(h).wait()

        def end_step(j, c, h=h):
            d = offset(j)
            z = lax.rem(me_z + d, peers)
            for which in range(3):
                a2a(which, h, d, z).wait_send()
            result(h, z).wait_send()
            result_arrival(h, z).wait_recv()
            return c

        lax.fori_loop(1, peers - 1, end_step, 0)
        result_arrival(h, opposite).wait_recv()
        for which in range(4):
            for side in range(2):
                hop(which, h, side).wait_send()
                pass_on(which, h, side).wait_send()

        def halo_end(z, c, h=h):
            for side in range(2):
                halo(h, z, side).wait_send()
            return c

        lax.fori_loop(0, peers, halo_end, 0)


def per_device(queries, key_tokens, value_tokens, text_keys, text_values, text_length):
    shape = queries.shape
    features = shape[3]
    cells = shape[0] * shape[1] * shape[2]
    peers = lax.axis_size("height")
    frames_axis = lax.axis_size("tm")
    heads = features // DH // peers
    text_rows = text_keys.shape[0]
    flat = [x.reshape(cells, features) for x in (queries, key_tokens, value_tokens)]
    any_space = pl.BlockSpec(memory_space=pl.ANY)
    vmem = pl.BlockSpec(memory_space=pltpu.VMEM)
    dma = pltpu.SemaphoreType.DMA
    result = pl.pallas_call(
        functools.partial(kernel, peers, frames_axis, heads, cells, text_rows),
        out_shape=jax.ShapeDtypeStruct((cells, features), jnp.bfloat16),
        in_specs=[any_space] * 3 + [vmem] * 2 + [pl.BlockSpec(memory_space=pltpu.SMEM)],
        out_specs=any_space,
        scratch_shapes=[
            pltpu.VMEM((3, heads, peers, 2, cells, DH), jnp.bfloat16),
            pltpu.VMEM((heads, peers, cells, DH), jnp.bfloat16),
            pltpu.VMEM((heads, peers, cells, DH), jnp.bfloat16),
            pltpu.VMEM((heads, 4, 2, cells // 2, DH), jnp.bfloat16),
            pltpu.VMEM((frames_axis, text_rows, 2 * heads * DH), jnp.float32),
            pltpu.VMEM((heads, frames_axis * text_rows, DH), jnp.bfloat16),
            pltpu.VMEM((heads, frames_axis * text_rows, DH), jnp.bfloat16),
            pltpu.VMEM((ZT * cells, frames_axis * text_rows), jnp.float32),
            pltpu.VMEM((3, ZT * cells, 3 * ZT * cells), jnp.float32),
            pltpu.VMEM((3, ZT * cells, 3 * ZT * cells), jnp.bfloat16),
            dma((heads, 3, peers)),
            dma((heads, 3, peers)),
            dma((heads, 2, peers)),
            dma((heads, 2, peers)),
            dma((heads, peers)),
            dma((heads, peers)),
            dma((heads, 4, 2)),
            dma((heads, 4, 2)),
            dma((heads, 4, 2)),
            dma,
            dma,
            dma((heads, 3)),
        ],
        compiler_params=pltpu.CompilerParams(
            collective_id=0, has_side_effects=True, vmem_limit_bytes=62 * 1024 * 1024
        ),
        cost_estimate=pl.CostEstimate(
            flops=5_000_000_000, bytes_accessed=4_000_000, transcendentals=10_000_000
        ),
    )(*flat, text_keys, text_values, text_length)
    return result.reshape(shape)


def solution(mesh):
    placed = (
        P(("rep", "tm"), "height", None, None),
        P(("rep", "tm"), "height", None, None),
        P(("rep", "tm"), "height", None, None),
        P(("rep", "tm"), "height"),
        P(("rep", "tm"), "height"),
        P("rep"),
    )
    return jax.shard_map(
        per_device,
        mesh=mesh,
        in_specs=placed,
        out_specs=P(("rep", "tm"), "height", None, None),
        check_vma=False,
    )
```

```python
import functools
import math

import jax
import jax.numpy as jnp
from jax import lax
from jax.experimental import pallas as pl
from jax.experimental.pallas import tpu as pltpu
from jax.sharding import PartitionSpec as P

DH = 128
ZT = 2
LOG2E = 1.4426950408889634


def kernel(
    peers,
    frames_axis,
    heads,
    cells,
    text_rows,
    q_ref,
    k_ref,
    v_ref,
    tk_ref,
    tv_ref,
    len_ref,
    out_ref,
    kv,
    qh,
    oh,
    text,
    text_k,
    text_v,
    text_s,
    scores,
    weights,
    a2a_send,
    a2a_recv,
    halo_send,
    halo_recv,
    out_send,
    out_recv,
    text_send,
    text_recv,
    local_sem,
):
    me_t = lax.axis_index("tm")
    me_z = lax.axis_index("height")
    tiles = peers // ZT
    nxt = lax.rem(me_t + 1, frames_axis)
    prv = lax.rem(me_t + frames_axis - 1, frames_axis)

    def offset(j):
        return jnp.where(lax.rem(j, 2) == 1, (j + 1) // 2, peers - j // 2)

    def columns(z, h):
        return pl.ds(pl.multiple_of((z * heads + h) * DH, DH), DH)

    barrier = pltpu.get_barrier_semaphore()

    def greet_z(j, c):
        pl.semaphore_signal(barrier, inc=1, device_id={"height": lax.rem(me_z + j, peers)})
        return c

    def greet_t(j, c):
        pl.semaphore_signal(barrier, inc=1, device_id={"tm": lax.rem(me_t + j, frames_axis)})
        return c

    lax.fori_loop(1, peers, greet_z, 0)
    lax.fori_loop(1, frames_axis, greet_t, 0)
    pl.semaphore_wait(barrier, peers - 1 + frames_axis - 1)

    sources = (k_ref, v_ref, q_ref)

    def landing(which, h, z):
        return qh.at[h, z] if which == 2 else kv.at[1, h, z, which]

    def a2a(which, h, d, z):
        return pltpu.make_async_remote_copy(
            src_ref=sources[which].at[:, columns(z, h)],
            dst_ref=landing(which, h, me_z),
            send_sem=a2a_send.at[h, which, d],
            recv_sem=a2a_recv.at[h, which, d],
            device_id={"height": z},
        )

    def arrival(which, h, d, z):
        return pltpu.make_async_remote_copy(
            src_ref=sources[which].at[:, columns(z, h)],
            dst_ref=landing(which, h, z),
            send_sem=a2a_send.at[h, which, d],
            recv_sem=a2a_recv.at[h, which, d],
            device_id={"height": z},
        )

    def own(which, h):
        return pltpu.make_async_copy(
            sources[which].at[:, columns(me_z, h)], landing(which, h, me_z), local_sem.at[h, which]
        )

    def send(which_list, h, d):
        z = lax.rem(me_z + d, peers)
        for which in which_list:
            a2a(which, h, d, z).start()

    def send_all(which_list, h):
        def step(j, c):
            send(which_list, h, offset(j))
            return c

        lax.fori_loop(1, peers, step, 0)

    def halo(h, z, side):
        return pltpu.make_async_remote_copy(
            src_ref=kv.at[1, h, z],
            dst_ref=kv.at[2 * side, h, z],
            send_sem=halo_send.at[h, side, z],
            recv_sem=halo_recv.at[h, side, z],
            device_id={"tm": nxt if side == 0 else prv},
        )

    def forward(h, beside):
        for which in range(2):
            own(which, h).wait()
        for side in range(2):
            halo(h, me_z, side).start()

        def step(j, c):
            d = offset(j)
            z = lax.rem(me_z + peers - d, peers)
            beside(j)
            for which in range(2):
                arrival(which, h, d, z).wait_recv()
            for side in range(2):
                halo(h, z, side).start()
            return c

        lax.fori_loop(1, peers, step, 0)

    def send_text(j):
        pltpu.make_async_remote_copy(
            src_ref=text.at[me_t],
            dst_ref=text.at[me_t],
            send_sem=text_send,
            recv_sem=text_recv,
            device_id={"tm": lax.rem(me_t + j, frames_axis)},
        ).start()

    share = -(-(frames_axis - 1) // (peers - 1))

    def beside_first(j):
        send((0, 1), 1, offset(j))

        def step(i, c):
            send_text(i)
            return c

        start = 1 + (j - 1) * share
        lax.fori_loop(start, jnp.minimum(start + share, frames_axis), step, 0)

    def beside_last(j):
        send((2,), 0, offset(peers - j))

    for h in range(heads):
        for which in range(3):
            own(which, h).start()
    send_all((0, 1), 0)
    own_text = [tk_ref[...].astype(jnp.float32), tv_ref[...].astype(jnp.float32)]
    text[me_t] = jnp.concatenate(own_text, 0).astype(jnp.bfloat16)
    forward(0, beside_first)
    forward(1, beside_last)

    def last_queries(j, c):
        send((2,), 1, offset(peers - j))
        return c

    lax.fori_loop(1, peers, last_queries, 0)
    rest = text.at[pl.ds(1, frames_axis - 1)]
    all_text = pltpu.make_async_remote_copy(
        src_ref=rest, dst_ref=rest, send_sem=text_send, recv_sem=text_recv, device_id={"tm": nxt}
    )
    all_text.wait()
    for h in range(heads):
        both = text[:, :, h * DH : (h + 1) * DH].astype(jnp.float32)
        text_k[h] = both[:, :text_rows].reshape(-1, DH).astype(jnp.bfloat16)
        text_v[h] = both[:, text_rows:].reshape(-1, DH).astype(jnp.bfloat16)

    scale = LOG2E / math.sqrt(DH)
    rows = ZT * cells
    bias = (
        jnp.where(me_t == 0, -jnp.inf, 0.0).astype(jnp.float32),
        jnp.float32(0.0),
        jnp.where(me_t == frames_axis - 1, -jnp.inf, 0.0).astype(jnp.float32),
    )
    ones = jnp.ones((3 * ZT * cells, DH), jnp.bfloat16)

    def product(q, k):
        return lax.dot_general(q, k, (((1,), (1,)), ((), ())), preferred_element_type=jnp.float32)

    def lanes_max(s):
        parts = [s[:, i : i + DH] for i in range(0, s.shape[1], DH)]
        return functools.reduce(jnp.maximum, parts)

    def weights_of(s, shift):
        parts = [
            jnp.exp2(s[:, i : i + DH] * scale - shift).astype(jnp.bfloat16)
            for i in range(0, s.shape[1], DH)
        ]
        return jnp.concatenate(parts, 1)

    def tile(h, a, start, count):
        n = count * cells
        chunks = [(c, min(256, n - c)) for c in range(0, n, 256)]
        q = qh[h, pl.ds(ZT * a, ZT)].reshape(rows, DH)
        s = product(q, text_k[h])
        place = lax.broadcasted_iota(jnp.int32, s.shape, 1)
        s = jnp.where(place < len_ref[0], s, -jnp.inf)
        text_s[...] = s
        top = lanes_max(s)
        for t in range(3):
            k = kv[t, h, pl.ds(start, count), 0].reshape(n, DH)
            part = None
            for c, w in chunks:
                s = product(q, k[c : c + w])
                scores[t, :, c : c + w] = s
                m = lanes_max(s)
                part = m if part is None else jnp.maximum(part, m)
            top = jnp.maximum(top, part + bias[t])
        top = jnp.broadcast_to(jnp.max(top, 1, keepdims=True) * scale, (rows, DH))

        acc = jnp.dot(
            weights_of(text_s[...], top),
            jnp.concatenate([text_v[h], ones[: text_v.shape[1]]], 1),
            preferred_element_type=jnp.float32,
        )
        for t in range(3):
            shift = top - bias[t]
            for c, w in chunks:
                weights[t, :, c : c + w] = weights_of(scores[t, :, c : c + w], shift)
            v = kv[t, h, pl.ds(start, count), 1].reshape(n, DH)
            acc = acc + jnp.dot(
                weights[t, :, :n],
                jnp.concatenate([v, ones[:n]], 1),
                preferred_element_type=jnp.float32,
            )
        oh[h, pl.ds(ZT * a, ZT)] = (
            (acc[:, :DH] / acc[:, DH:]).astype(jnp.bfloat16).reshape(ZT, cells, DH)
        )

    def result(h, z):
        return pltpu.make_async_remote_copy(
            src_ref=oh.at[h, z],
            dst_ref=out_ref.at[:, columns(me_z, h)],
            send_sem=out_send.at[h, z],
            recv_sem=out_recv.at[h, me_z],
            device_id={"height": z},
        )

    def result_own(h):
        return pltpu.make_async_copy(
            oh.at[h, me_z], out_ref.at[:, columns(me_z, h)], out_send.at[h, me_z]
        )

    def send_tile(h, a):
        for i in range(ZT):
            z = ZT * a + i

            @pl.when(z != me_z)
            def _():
                result(h, z).start()

            @pl.when(z == me_z)
            def _():
                result_own(h).start()

    def wait_queries(h, a):
        for i in range(ZT):
            z = ZT * a + i

            @pl.when(z != me_z)
            def _():
                arrival(2, h, lax.rem(me_z + peers - z, peers), z).wait_recv()

            @pl.when(z == me_z)
            def _():
                own(2, h).wait()

    for h in range(heads):
        def halo_step(z, c, h=h):
            for side in range(2):
                halo(h, z, side).wait_recv()
            return c

        lax.fori_loop(0, peers, halo_step, 0)

        def tile_step(i, c, h=h):
            side = 1 + 2 * lax.rem(me_t, 2)
            ahead = jnp.where(i == 0, 2, jnp.where(i == 1, side, jnp.where(i == 2, 4 - side, 0)))
            a = lax.rem(me_z // ZT + ahead, tiles)
            low = a == 0
            at_edge = jnp.logical_or(low, a == tiles - 1)
            wait_queries(h, a)

            @pl.when(at_edge)
            def _():
                tile(h, a, jnp.where(low, 0, (tiles - 2) * ZT), 2 * ZT)

            @pl.when(jnp.logical_not(at_edge))
            def _():
                tile(h, a, (a - 1) * ZT, 3 * ZT)

            send_tile(h, a)
            return c

        lax.fori_loop(0, tiles, tile_step, 0)

    for h in range(heads):
        result_own(h).wait()

        def end_step(j, c, h=h):
            d = offset(j)
            z = lax.rem(me_z + d, peers)
            for which in range(3):
                a2a(which, h, d, z).wait_send()
            result(h, z).wait_send()
            pltpu.make_async_remote_copy(
                src_ref=oh.at[h, z],
                dst_ref=out_ref.at[:, columns(z, h)],
                send_sem=out_send.at[h, z],
                recv_sem=out_recv.at[h, z],
                device_id={"height": z},
            ).wait_recv()
            return c

        lax.fori_loop(1, peers, end_step, 0)

        def halo_end(z, c, h=h):
            for side in range(2):
                halo(h, z, side).wait_send()
            return c

        lax.fori_loop(0, peers, halo_end, 0)


def per_device(queries, key_tokens, value_tokens, text_keys, text_values, text_length):
    shape = queries.shape
    features = shape[3]
    cells = shape[0] * shape[1] * shape[2]
    peers = lax.axis_size("height")
    frames_axis = lax.axis_size("tm")
    heads = features // DH // peers
    text_rows = text_keys.shape[0]
    flat = [x.reshape(cells, features) for x in (queries, key_tokens, value_tokens)]
    any_space = pl.BlockSpec(memory_space=pl.ANY)
    vmem = pl.BlockSpec(memory_space=pltpu.VMEM)
    dma = pltpu.SemaphoreType.DMA
    result = pl.pallas_call(
        functools.partial(kernel, peers, frames_axis, heads, cells, text_rows),
        out_shape=jax.ShapeDtypeStruct((cells, features), jnp.bfloat16),
        in_specs=[any_space] * 3 + [vmem] * 2 + [pl.BlockSpec(memory_space=pltpu.SMEM)],
        out_specs=any_space,
        scratch_shapes=[
            pltpu.VMEM((3, heads, peers, 2, cells, DH), jnp.bfloat16),
            pltpu.VMEM((heads, peers, cells, DH), jnp.bfloat16),
            pltpu.VMEM((heads, peers, cells, DH), jnp.bfloat16),
            pltpu.VMEM((frames_axis, 2 * text_rows, heads * DH), jnp.bfloat16),
            pltpu.VMEM((heads, frames_axis * text_rows, DH), jnp.bfloat16),
            pltpu.VMEM((heads, frames_axis * text_rows, DH), jnp.bfloat16),
            pltpu.VMEM((ZT * cells, frames_axis * text_rows), jnp.float32),
            pltpu.VMEM((3, ZT * cells, 3 * ZT * cells), jnp.float32),
            pltpu.VMEM((3, ZT * cells, 3 * ZT * cells), jnp.bfloat16),
            dma((heads, 3, peers)),
            dma((heads, 3, peers)),
            dma((heads, 2, peers)),
            dma((heads, 2, peers)),
            dma((heads, peers)),
            dma((heads, peers)),
            dma,
            dma,
            dma((heads, 3)),
        ],
        compiler_params=pltpu.CompilerParams(
            collective_id=0, has_side_effects=True, vmem_limit_bytes=62 * 1024 * 1024
        ),
        cost_estimate=pl.CostEstimate(
            flops=5_000_000_000, bytes_accessed=4_000_000, transcendentals=10_000_000
        ),
    )(*flat, text_keys, text_values, text_length)
    return result.reshape(shape)


def solution(mesh):
    placed = (
        P(("rep", "tm"), "height", None, None),
        P(("rep", "tm"), "height", None, None),
        P(("rep", "tm"), "height", None, None),
        P(("rep", "tm"), "height"),
        P(("rep", "tm"), "height"),
        P("rep"),
    )
    return jax.shard_map(
        per_device,
        mesh=mesh,
        in_specs=placed,
        out_specs=P(("rep", "tm"), "height", None, None),
        check_vma=False,
    )
```

```python
import functools
import math

import jax
import jax.numpy as jnp
from jax import lax
from jax.experimental import pallas as pl
from jax.experimental.pallas import tpu as pltpu
from jax.sharding import PartitionSpec as P

DH = 128
ZT = 2
LOG2E = 1.4426950408889634


def kernel(
    peers,
    frames_axis,
    heads,
    cells,
    text_rows,
    q_ref,
    k_ref,
    v_ref,
    tk_ref,
    tv_ref,
    len_ref,
    out_ref,
    kv,
    qh,
    oh,
    text,
    text_k,
    text_v,
    text_s,
    scores,
    a2a_send,
    a2a_recv,
    halo_send,
    halo_recv,
    out_send,
    out_recv,
    text_send,
    text_recv,
    local_sem,
):
    me_t = lax.axis_index("tm")
    me_z = lax.axis_index("height")
    tiles = peers // ZT
    nxt = lax.rem(me_t + 1, frames_axis)
    prv = lax.rem(me_t + frames_axis - 1, frames_axis)

    def offset(j):
        return jnp.where(lax.rem(j, 2) == 1, (j + 1) // 2, peers - j // 2)

    def columns(z, h):
        return pl.ds(pl.multiple_of((z * heads + h) * DH, DH), DH)

    barrier = pltpu.get_barrier_semaphore()

    def greet_z(j, c):
        pl.semaphore_signal(barrier, inc=1, device_id={"height": lax.rem(me_z + j, peers)})
        return c

    def greet_t(j, c):
        pl.semaphore_signal(barrier, inc=1, device_id={"tm": lax.rem(me_t + j, frames_axis)})
        return c

    lax.fori_loop(1, peers, greet_z, 0)
    lax.fori_loop(1, frames_axis, greet_t, 0)
    pl.semaphore_wait(barrier, peers - 1 + frames_axis - 1)

    sources = (k_ref, v_ref, q_ref)

    def landing(which, h, z):
        return qh.at[h, z] if which == 2 else kv.at[1, h, z, which]

    def a2a(which, h, d, z):
        return pltpu.make_async_remote_copy(
            src_ref=sources[which].at[:, columns(z, h)],
            dst_ref=landing(which, h, me_z),
            send_sem=a2a_send.at[h, which, d],
            recv_sem=a2a_recv.at[h, which, d],
            device_id={"height": z},
        )

    def arrival(which, h, d, z):
        return pltpu.make_async_remote_copy(
            src_ref=sources[which].at[:, columns(z, h)],
            dst_ref=landing(which, h, z),
            send_sem=a2a_send.at[h, which, d],
            recv_sem=a2a_recv.at[h, which, d],
            device_id={"height": z},
        )

    def own(which, h):
        return pltpu.make_async_copy(
            sources[which].at[:, columns(me_z, h)], landing(which, h, me_z), local_sem.at[h, which]
        )

    def send(which_list, h, d):
        z = lax.rem(me_z + d, peers)
        for which in which_list:
            a2a(which, h, d, z).start()

    def send_all(which_list, h):
        def step(j, c):
            send(which_list, h, offset(j))
            return c

        lax.fori_loop(1, peers, step, 0)

    def halo(h, z, side):
        return pltpu.make_async_remote_copy(
            src_ref=kv.at[1, h, z],
            dst_ref=kv.at[2 * side, h, z],
            send_sem=halo_send.at[h, side, z],
            recv_sem=halo_recv.at[h, side, z],
            device_id={"tm": nxt if side == 0 else prv},
        )

    def forward_own(h):
        for which in range(2):
            own(which, h).wait()
        for side in range(2):
            halo(h, me_z, side).start()

    def forward(h, beside, first, end):
        def step(j, c):
            d = offset(j)
            z = lax.rem(me_z + peers - d, peers)
            beside(j)
            for which in range(2):
                arrival(which, h, d, z).wait_recv()
            for side in range(2):
                halo(h, z, side).start()
            return c

        lax.fori_loop(first, end, step, 0)

    def send_text(j):
        pltpu.make_async_remote_copy(
            src_ref=text.at[me_t],
            dst_ref=text.at[me_t],
            send_sem=text_send,
            recv_sem=text_recv,
            device_id={"tm": lax.rem(me_t + j, frames_axis)},
        ).start()

    share = -(-(frames_axis - 1) // (peers - 1))

    def beside_first(j):
        send((0, 1), 1, offset(j))

        def step(i, c):
            send_text(i)
            return c

        start = 1 + (j - 1) * share
        lax.fori_loop(start, jnp.minimum(start + share, frames_axis), step, 0)

    def beside_last(j):
        send((2,), 1, offset(peers - j))

    for h in range(heads):
        for which in range(3):
            own(which, h).start()
    send_all((0, 1), 0)
    own_text = [tk_ref[...].astype(jnp.float32), tv_ref[...].astype(jnp.float32)]
    text[me_t] = jnp.concatenate(own_text, 0).astype(jnp.bfloat16)

    def first_queries(j, c):
        send((2,), 0, offset(peers - j))
        return c

    lax.fori_loop(1, peers, first_queries, 0)
    forward_own(0)
    forward(0, beside_first, 1, peers)
    forward_own(1)

    rest = text.at[pl.ds(1, frames_axis - 1)]
    all_text = pltpu.make_async_remote_copy(
        src_ref=rest, dst_ref=rest, send_sem=text_send, recv_sem=text_recv, device_id={"tm": nxt}
    )
    all_text.wait()
    for h in range(heads):
        both = text[:, :, h * DH : (h + 1) * DH].astype(jnp.float32)
        text_k[h] = both[:, :text_rows].reshape(-1, DH).astype(jnp.bfloat16)
        text_v[h] = both[:, text_rows:].reshape(-1, DH).astype(jnp.bfloat16)

    scale = LOG2E / math.sqrt(DH)
    rows = ZT * cells
    bias = (
        jnp.where(me_t == 0, -jnp.inf, 0.0).astype(jnp.float32),
        jnp.float32(0.0),
        jnp.where(me_t == frames_axis - 1, -jnp.inf, 0.0).astype(jnp.float32),
    )
    ones = jnp.ones((3 * ZT * cells, DH), jnp.bfloat16)

    def product(q, k):
        return lax.dot_general(q, k, (((1,), (1,)), ((), ())), preferred_element_type=jnp.float32)

    def lanes_max(s):
        parts = [s[:, i : i + DH] for i in range(0, s.shape[1], DH)]
        return functools.reduce(jnp.maximum, parts)

    def weights_of(s, shift):
        parts = [
            jnp.exp2(s[:, i : i + DH] * scale - shift).astype(jnp.bfloat16)
            for i in range(0, s.shape[1], DH)
        ]
        return jnp.concatenate(parts, 1)

    def tile(h, a, start, count):
        n = count * cells
        chunks = [(c, min(256, n - c)) for c in range(0, n, 256)]
        wide_chunks = [(0, 512), (512, n - 512)]
        q = qh[h, pl.ds(ZT * a, ZT)].reshape(rows, DH)
        s = product(q, text_k[h])
        place = lax.broadcasted_iota(jnp.int32, s.shape, 1)
        s = jnp.where(place < len_ref[0], s, -jnp.inf)
        text_s[...] = s
        top = lanes_max(s)
        for t in range(3):
            k = kv[t, h, pl.ds(start, count), 0].reshape(n, DH)
            part = None
            for c, w in chunks:
                s = product(q, k[c : c + w])
                scores[t, :, c : c + w] = s
                m = lanes_max(s)
                part = m if part is None else jnp.maximum(part, m)
            top = jnp.maximum(top, part + bias[t])
        top = jnp.broadcast_to(jnp.max(top, 1, keepdims=True) * scale, (rows, DH))

        pieces = [(t, c, w) for t in range(3) for c, w in wide_chunks]
        values = [kv[t, h, pl.ds(start, count), 1].reshape(n, DH) for t in range(3)]
        shifts = [top - b for b in bias]

        def value_product(p, v):
            both = jnp.concatenate([v, ones[: v.shape[0]]], 1)
            return jnp.dot(p, both, preferred_element_type=jnp.float32)

        acc = None
        held = weights_of(text_s[...], top)
        held_v = text_v[h]
        for t, c, w in pieces:
            p = weights_of(scores[t, :, c : c + w], shifts[t])
            part = value_product(held, held_v)
            acc = part if acc is None else acc + part
            held, held_v = p, values[t][c : c + w]
        acc = acc + value_product(held, held_v)
        oh[h, pl.ds(ZT * a, ZT)] = (
            (acc[:, :DH] / acc[:, DH:]).astype(jnp.bfloat16).reshape(ZT, cells, DH)
        )

    def result(h, z):
        return pltpu.make_async_remote_copy(
            src_ref=oh.at[h, z],
            dst_ref=out_ref.at[:, columns(me_z, h)],
            send_sem=out_send.at[h, z],
            recv_sem=out_recv.at[h, me_z],
            device_id={"height": z},
        )

    def result_own(h):
        return pltpu.make_async_copy(
            oh.at[h, me_z], out_ref.at[:, columns(me_z, h)], out_send.at[h, me_z]
        )

    def send_tile(h, a):
        for i in range(ZT):
            z = ZT * a + i

            @pl.when(z != me_z)
            def _():
                result(h, z).start()

            @pl.when(z == me_z)
            def _():
                result_own(h).start()

    def wait_queries(h, a):
        for i in range(ZT):
            z = ZT * a + i

            @pl.when(z != me_z)
            def _():
                arrival(2, h, lax.rem(me_z + peers - z, peers), z).wait_recv()

            @pl.when(z == me_z)
            def _():
                own(2, h).wait()

    for h in range(heads):
        def halo_step(z, c, h=h):
            for side in range(2):
                halo(h, z, side).wait_recv()
            return c

        lax.fori_loop(0, peers, halo_step, 0)

        def tile_step(i, c, h=h):
            side = 1 + 2 * lax.rem(me_t, 2)
            ahead = jnp.where(i == 0, 2, jnp.where(i == 1, side, jnp.where(i == 2, 4 - side, 0)))
            a = lax.rem(me_z // ZT + ahead, tiles)
            low = a == 0
            at_edge = jnp.logical_or(low, a == tiles - 1)
            wait_queries(h, a)

            @pl.when(at_edge)
            def _():
                tile(h, a, jnp.where(low, 0, (tiles - 2) * ZT), 2 * ZT)

            @pl.when(jnp.logical_not(at_edge))
            def _():
                tile(h, a, (a - 1) * ZT, 3 * ZT)

            send_tile(h, a)
            if h == 0:
                begin = 1 + 2 * i
                forward(1, beside_last, begin, jnp.minimum(begin + 2, peers))
            return c

        lax.fori_loop(0, tiles, tile_step, 0)

    for h in range(heads):
        result_own(h).wait()

        def end_step(j, c, h=h):
            d = offset(j)
            z = lax.rem(me_z + d, peers)
            for which in range(3):
                a2a(which, h, d, z).wait_send()
            result(h, z).wait_send()
            pltpu.make_async_remote_copy(
                src_ref=oh.at[h, z],
                dst_ref=out_ref.at[:, columns(z, h)],
                send_sem=out_send.at[h, z],
                recv_sem=out_recv.at[h, z],
                device_id={"height": z},
            ).wait_recv()
            return c

        lax.fori_loop(1, peers, end_step, 0)

        def halo_end(z, c, h=h):
            for side in range(2):
                halo(h, z, side).wait_send()
            return c

        lax.fori_loop(0, peers, halo_end, 0)


def per_device(queries, key_tokens, value_tokens, text_keys, text_values, text_length):
    shape = queries.shape
    features = shape[3]
    cells = shape[0] * shape[1] * shape[2]
    peers = lax.axis_size("height")
    frames_axis = lax.axis_size("tm")
    heads = features // DH // peers
    text_rows = text_keys.shape[0]
    flat = [x.reshape(cells, features) for x in (queries, key_tokens, value_tokens)]
    any_space = pl.BlockSpec(memory_space=pl.ANY)
    vmem = pl.BlockSpec(memory_space=pltpu.VMEM)
    dma = pltpu.SemaphoreType.DMA
    result = pl.pallas_call(
        functools.partial(kernel, peers, frames_axis, heads, cells, text_rows),
        out_shape=jax.ShapeDtypeStruct((cells, features), jnp.bfloat16),
        in_specs=[any_space] * 3 + [vmem] * 2 + [pl.BlockSpec(memory_space=pltpu.SMEM)],
        out_specs=any_space,
        scratch_shapes=[
            pltpu.VMEM((3, heads, peers, 2, cells, DH), jnp.bfloat16),
            pltpu.VMEM((heads, peers, cells, DH), jnp.bfloat16),
            pltpu.VMEM((heads, peers, cells, DH), jnp.bfloat16),
            pltpu.VMEM((frames_axis, 2 * text_rows, heads * DH), jnp.bfloat16),
            pltpu.VMEM((heads, frames_axis * text_rows, DH), jnp.bfloat16),
            pltpu.VMEM((heads, frames_axis * text_rows, DH), jnp.bfloat16),
            pltpu.VMEM((ZT * cells, frames_axis * text_rows), jnp.float32),
            pltpu.VMEM((3, ZT * cells, 3 * ZT * cells), jnp.float32),
            dma((heads, 3, peers)),
            dma((heads, 3, peers)),
            dma((heads, 2, peers)),
            dma((heads, 2, peers)),
            dma((heads, peers)),
            dma((heads, peers)),
            dma,
            dma,
            dma((heads, 3)),
        ],
        compiler_params=pltpu.CompilerParams(
            collective_id=0, has_side_effects=True, vmem_limit_bytes=62 * 1024 * 1024
        ),
        cost_estimate=pl.CostEstimate(
            flops=5_000_000_000, bytes_accessed=4_000_000, transcendentals=10_000_000
        ),
    )(*flat, text_keys, text_values, text_length)
    return result.reshape(shape)


def solution(mesh):
    placed = (
        P(("rep", "tm"), "height", None, None),
        P(("rep", "tm"), "height", None, None),
        P(("rep", "tm"), "height", None, None),
        P(("rep", "tm"), "height"),
        P(("rep", "tm"), "height"),
        P("rep"),
    )
    return jax.shard_map(
        per_device,
        mesh=mesh,
        in_specs=placed,
        out_specs=P(("rep", "tm"), "height", None, None),
        check_vma=False,
    )
```

```python
import functools
import math

import jax
import jax.numpy as jnp
from jax import lax
from jax.experimental import pallas as pl
from jax.experimental.pallas import tpu as pltpu
from jax.sharding import PartitionSpec as P

DH = 128
ZT = 2
LOG2E = 1.4426950408889634


def kernel(
    peers,
    frames_axis,
    heads,
    cells,
    text_rows,
    q_ref,
    k_ref,
    v_ref,
    tk_ref,
    tv_ref,
    len_ref,
    out_ref,
    kv,
    qh,
    oh,
    relay,
    text,
    text_k,
    text_v,
    text_s,
    scores,
    a2a_send,
    a2a_recv,
    halo_send,
    halo_recv,
    out_send,
    out_recv,
    hop_send,
    hop_recv,
    pass_send,
    text_send,
    text_recv,
    local_sem,
):
    me_t = lax.axis_index("tm")
    me_z = lax.axis_index("height")
    tiles = peers // ZT
    nxt = lax.rem(me_t + 1, frames_axis)
    prv = lax.rem(me_t + frames_axis - 1, frames_axis)

    pairs = peers // 2 - 1

    def offsets(p):
        first = jnp.where(lax.rem(me_t, 2) == 0, p, peers - p)
        return first, peers - first

    def columns(z, h):
        return pl.ds(pl.multiple_of((z * heads + h) * DH, DH), DH)

    barrier = pltpu.get_barrier_semaphore()

    def greet_z(j, c):
        pl.semaphore_signal(barrier, inc=1, device_id={"height": lax.rem(me_z + j, peers)})
        return c

    def greet_t(j, c):
        pl.semaphore_signal(barrier, inc=1, device_id={"tm": lax.rem(me_t + j, frames_axis)})
        return c

    lax.fori_loop(1, peers, greet_z, 0)
    lax.fori_loop(1, frames_axis, greet_t, 0)
    pl.semaphore_wait(barrier, peers - 1 + frames_axis - 1)

    sources = (k_ref, v_ref, q_ref)

    def landing(which, h, z):
        return qh.at[h, z] if which == 2 else kv.at[1, h, z, which]

    def a2a(which, h, d, z):
        return pltpu.make_async_remote_copy(
            src_ref=sources[which].at[:, columns(z, h)],
            dst_ref=landing(which, h, me_z),
            send_sem=a2a_send.at[h, which, d],
            recv_sem=a2a_recv.at[h, which, d],
            device_id={"height": z},
        )

    def arrival(which, h, d, z):
        return pltpu.make_async_remote_copy(
            src_ref=sources[which].at[:, columns(z, h)],
            dst_ref=landing(which, h, z),
            send_sem=a2a_send.at[h, which, d],
            recv_sem=a2a_recv.at[h, which, d],
            device_id={"height": z},
        )

    def own(which, h):
        return pltpu.make_async_copy(
            sources[which].at[:, columns(me_z, h)], landing(which, h, me_z), local_sem.at[h, which]
        )

    opposite = lax.rem(me_z + peers // 2, peers)

    def half(side):
        return pl.ds(side * (cells // 2), cells // 2)

    def shifted(by):
        return lax.rem(me_z + peers + by, peers)

    def hop(which, h, side):
        if which == 3:
            source = oh.at[h, opposite, half(side)]
        else:
            source = sources[which].at[half(side), columns(opposite, h)]
        return pltpu.make_async_remote_copy(
            src_ref=source,
            dst_ref=relay.at[h, which, side],
            send_sem=hop_send.at[h, which, side],
            recv_sem=hop_recv.at[h, which, side],
            device_id={"height": shifted(1 - 2 * side)},
        )

    def pass_on(which, h, side):
        origin = shifted(2 * side - 1)
        if which == 3:
            target, counted = out_ref.at[half(side), columns(origin, h)], out_recv.at[h, origin]
        else:
            counted = a2a_recv.at[h, which, peers // 2]
            if which == 2:
                target = qh.at[h, origin, half(side)]
            else:
                target = kv.at[1, h, origin, which, half(side)]
        return pltpu.make_async_remote_copy(
            src_ref=relay.at[h, which, side],
            dst_ref=target,
            send_sem=pass_send.at[h, which, side],
            recv_sem=counted,
            device_id={"height": shifted((1 - 2 * side) * (peers // 2 - 1))},
        )

    def relay_step(which, h):
        for side in range(2):
            hop(which, h, side).wait_recv()
            pass_on(which, h, side).start()

    def start_hops(which_list, h):
        for which in which_list:
            for side in range(2):
                hop(which, h, side).start()

    def send_pair(which_list, h, p):
        for which in which_list:
            for d in offsets(p):
                a2a(which, h, d, lax.rem(me_z + d, peers)).start()

    def halo(h, z, side):
        return pltpu.make_async_remote_copy(
            src_ref=kv.at[1, h, z],
            dst_ref=kv.at[2 * side, h, z],
            send_sem=halo_send.at[h, side, z],
            recv_sem=halo_recv.at[h, side, z],
            device_id={"tm": nxt if side == 0 else prv},
        )

    def forward_own(h):
        for which in range(2):
            own(which, h).wait()
        for side in range(2):
            halo(h, me_z, side).start()

    def forward_from(h, d):
        z = lax.rem(me_z + peers - d, peers)
        for which in range(2):
            arrival(which, h, d, z).wait_recv()
        for side in range(2):
            halo(h, z, side).start()

    def forward(h, beside, p):
        beside(p)
        for d in offsets(p):
            forward_from(h, d)

    def send_text(j):
        pltpu.make_async_remote_copy(
            src_ref=text.at[me_t],
            dst_ref=text.at[me_t],
            send_sem=text_send,
            recv_sem=text_recv,
            device_id={"tm": lax.rem(me_t + j, frames_axis)},
        ).start()

    share = -(-(frames_axis - 1) // pairs)

    def beside_first(p):
        send_pair((0, 1), 1, p)

        def step(i, c):
            send_text(i)
            return c

        start = 1 + (p - 1) * share
        lax.fori_loop(start, jnp.minimum(start + share, frames_axis), step, 0)

    def beside_last(p):
        send_pair((2,), 1, pairs + 1 - p)

    for h in range(heads):
        for which in range(3):
            own(which, h).start()
    start_hops((0, 1, 2), 0)
    for p in range(1, pairs):
        send_pair((0, 1), 0, p)
    own_text = [tk_ref[...].astype(jnp.float32), tv_ref[...].astype(jnp.float32)]
    text[me_t] = jnp.concatenate(own_text, 0).astype(jnp.bfloat16)
    for which in range(3):
        relay_step(which, 0)
    send_pair((0, 1), 0, pairs)
    start_hops((0, 1, 2), 1)
    for p in range(pairs, 0, -1):
        send_pair((2,), 0, p)
    forward_own(0)

    def first_step(p, c):
        forward(0, beside_first, p)
        return c

    lax.fori_loop(1, pairs + 1, first_step, 0)
    forward_from(0, peers // 2)
    for which in range(3):
        relay_step(which, 1)
    forward_own(1)

    rest = text.at[pl.ds(1, frames_axis - 1)]
    all_text = pltpu.make_async_remote_copy(
        src_ref=rest, dst_ref=rest, send_sem=text_send, recv_sem=text_recv, device_id={"tm": nxt}
    )
    all_text.wait()
    for h in range(heads):
        both = text[:, :, h * DH : (h + 1) * DH].astype(jnp.float32)
        text_k[h] = both[:, :text_rows].reshape(-1, DH).astype(jnp.bfloat16)
        text_v[h] = both[:, text_rows:].reshape(-1, DH).astype(jnp.bfloat16)

    scale = LOG2E / math.sqrt(DH)
    rows = ZT * cells
    bias = (
        jnp.where(me_t == 0, -jnp.inf, 0.0).astype(jnp.float32),
        jnp.float32(0.0),
        jnp.where(me_t == frames_axis - 1, -jnp.inf, 0.0).astype(jnp.float32),
    )
    ones = jnp.ones((3 * ZT * cells, DH), jnp.bfloat16)

    def product(q, k):
        return lax.dot_general(q, k, (((1,), (1,)), ((), ())), preferred_element_type=jnp.float32)

    def lanes_max(s):
        parts = [s[:, i : i + DH] for i in range(0, s.shape[1], DH)]
        return functools.reduce(jnp.maximum, parts)

    def weights_of(s, shift):
        parts = [
            jnp.exp2(s[:, i : i + DH] * scale - shift).astype(jnp.bfloat16)
            for i in range(0, s.shape[1], DH)
        ]
        return jnp.concatenate(parts, 1)

    def tile(h, a, start, count):
        n = count * cells
        chunks = [(c, min(256, n - c)) for c in range(0, n, 256)]
        wide_chunks = [(0, 512), (512, n - 512)]
        q = qh[h, pl.ds(ZT * a, ZT)].reshape(rows, DH)
        s = product(q, text_k[h])
        place = lax.broadcasted_iota(jnp.int32, s.shape, 1)
        s = jnp.where(place < len_ref[0], s, -jnp.inf)
        text_s[...] = s
        top = lanes_max(s)
        for t in range(3):
            k = kv[t, h, pl.ds(start, count), 0].reshape(n, DH)
            part = None
            for c, w in chunks:
                s = product(q, k[c : c + w])
                scores[t, :, c : c + w] = s
                m = lanes_max(s)
                part = m if part is None else jnp.maximum(part, m)
            top = jnp.maximum(top, part + bias[t])
        top = jnp.broadcast_to(jnp.max(top, 1, keepdims=True) * scale, (rows, DH))

        pieces = [(t, c, w) for t in range(3) for c, w in wide_chunks]
        values = [kv[t, h, pl.ds(start, count), 1].reshape(n, DH) for t in range(3)]
        shifts = [top - b for b in bias]

        def value_product(p, v):
            both = jnp.concatenate([v, ones[: v.shape[0]]], 1)
            return jnp.dot(p, both, preferred_element_type=jnp.float32)

        acc = None
        held = weights_of(text_s[...], top)
        held_v = text_v[h]
        for t, c, w in pieces:
            p = weights_of(scores[t, :, c : c + w], shifts[t])
            part = value_product(held, held_v)
            acc = part if acc is None else acc + part
            held, held_v = p, values[t][c : c + w]
        acc = acc + value_product(held, held_v)
        oh[h, pl.ds(ZT * a, ZT)] = (
            (acc[:, :DH] / acc[:, DH:]).astype(jnp.bfloat16).reshape(ZT, cells, DH)
        )

    def result(h, z):
        return pltpu.make_async_remote_copy(
            src_ref=oh.at[h, z],
            dst_ref=out_ref.at[:, columns(me_z, h)],
            send_sem=out_send.at[h, z],
            recv_sem=out_recv.at[h, me_z],
            device_id={"height": z},
        )

    def result_arrival(h, z):
        return pltpu.make_async_remote_copy(
            src_ref=oh.at[h, z],
            dst_ref=out_ref.at[:, columns(z, h)],
            send_sem=out_send.at[h, z],
            recv_sem=out_recv.at[h, z],
            device_id={"height": z},
        )

    def result_own(h):
        return pltpu.make_async_copy(
            oh.at[h, me_z], out_ref.at[:, columns(me_z, h)], out_send.at[h, me_z]
        )

    def send_tile(h, a):
        for i in range(ZT):
            z = ZT * a + i

            @pl.when(jnp.logical_and(z != me_z, z != opposite))
            def _():
                result(h, z).start()

            @pl.when(z == opposite)
            def _():
                start_hops((3,), h)

            @pl.when(z == me_z)
            def _():
                result_own(h).start()

    def wait_queries(h, a):
        for i in range(ZT):
            z = ZT * a + i

            @pl.when(z != me_z)
            def _():
                arrival(2, h, lax.rem(me_z + peers - z, peers), z).wait_recv()

            @pl.when(z == me_z)
            def _():
                own(2, h).wait()

    for h in range(heads):
        def halo_step(z, c, h=h):
            for side in range(2):
                halo(h, z, side).wait_recv()
            return c

        lax.fori_loop(0, peers, halo_step, 0)

        def tile_step(i, c, h=h):
            side = 1 + 2 * lax.rem(me_t, 2)
            ahead = jnp.where(i == 0, 2, jnp.where(i == 1, side, jnp.where(i == 2, 4 - side, 0)))
            a = lax.rem(me_z // ZT + ahead, tiles)
            low = a == 0
            at_edge = jnp.logical_or(low, a == tiles - 1)
            wait_queries(h, a)
            if h == 1:

                @pl.when(i == 1)
                def _():
                    relay_step(3, 0)

                @pl.when(i == 3)
                def _():
                    relay_step(3, 1)

            @pl.when(at_edge)
            def _():
                tile(h, a, jnp.where(low, 0, (tiles - 2) * ZT), 2 * ZT)

            @pl.when(jnp.logical_not(at_edge))
            def _():
                tile(h, a, (a - 1) * ZT, 3 * ZT)

            send_tile(h, a)
            if h == 0:
                @pl.when(i < pairs)
                def _():
                    forward(1, beside_last, i + 1)

                @pl.when(i == pairs)
                def _():
                    forward_from(1, peers // 2)
            return c

        lax.fori_loop(0, tiles, tile_step, 0)

    for h in range(heads):
        result_own(h).wait()

        def end_step(p, c, h=h):
            for d in offsets(p):
                z = lax.rem(me_z + d, peers)
                for which in range(3):
                    a2a(which, h, d, z).wait_send()
                result(h, z).wait_send()
                result_arrival(h, z).wait_recv()
            return c

        lax.fori_loop(1, pairs + 1, end_step, 0)
        result_arrival(h, opposite).wait_recv()
        for which in range(4):
            for side in range(2):
                hop(which, h, side).wait_send()
                pass_on(which, h, side).wait_send()

        def halo_end(z, c, h=h):
            for side in range(2):
                halo(h, z, side).wait_send()
            return c

        lax.fori_loop(0, peers, halo_end, 0)


def per_device(queries, key_tokens, value_tokens, text_keys, text_values, text_length):
    shape = queries.shape
    features = shape[3]
    cells = shape[0] * shape[1] * shape[2]
    peers = lax.axis_size("height")
    frames_axis = lax.axis_size("tm")
    heads = features // DH // peers
    text_rows = text_keys.shape[0]
    flat = [x.reshape(cells, features) for x in (queries, key_tokens, value_tokens)]
    any_space = pl.BlockSpec(memory_space=pl.ANY)
    vmem = pl.BlockSpec(memory_space=pltpu.VMEM)
    dma = pltpu.SemaphoreType.DMA
    result = pl.pallas_call(
        functools.partial(kernel, peers, frames_axis, heads, cells, text_rows),
        out_shape=jax.ShapeDtypeStruct((cells, features), jnp.bfloat16),
        in_specs=[any_space] * 3 + [vmem] * 2 + [pl.BlockSpec(memory_space=pltpu.SMEM)],
        out_specs=any_space,
        scratch_shapes=[
            pltpu.VMEM((3, heads, peers, 2, cells, DH), jnp.bfloat16),
            pltpu.VMEM((heads, peers, cells, DH), jnp.bfloat16),
            pltpu.VMEM((heads, peers, cells, DH), jnp.bfloat16),
            pltpu.VMEM((heads, 4, 2, cells // 2, DH), jnp.bfloat16),
            pltpu.VMEM((frames_axis, 2 * text_rows, heads * DH), jnp.bfloat16),
            pltpu.VMEM((heads, frames_axis * text_rows, DH), jnp.bfloat16),
            pltpu.VMEM((heads, frames_axis * text_rows, DH), jnp.bfloat16),
            pltpu.VMEM((ZT * cells, frames_axis * text_rows), jnp.float32),
            pltpu.VMEM((3, ZT * cells, 3 * ZT * cells), jnp.float32),
            dma((heads, 3, peers)),
            dma((heads, 3, peers)),
            dma((heads, 2, peers)),
            dma((heads, 2, peers)),
            dma((heads, peers)),
            dma((heads, peers)),
            dma((heads, 4, 2)),
            dma((heads, 4, 2)),
            dma((heads, 4, 2)),
            dma,
            dma,
            dma((heads, 3)),
        ],
        compiler_params=pltpu.CompilerParams(
            collective_id=0, has_side_effects=True, vmem_limit_bytes=62 * 1024 * 1024
        ),
        cost_estimate=pl.CostEstimate(
            flops=5_000_000_000, bytes_accessed=4_000_000, transcendentals=10_000_000
        ),
    )(*flat, text_keys, text_values, text_length)
    return result.reshape(shape)


def solution(mesh):
    placed = (
        P(("rep", "tm"), "height", None, None),
        P(("rep", "tm"), "height", None, None),
        P(("rep", "tm"), "height", None, None),
        P(("rep", "tm"), "height"),
        P(("rep", "tm"), "height"),
        P("rep"),
    )
    return jax.shard_map(
        per_device,
        mesh=mesh,
        in_specs=placed,
        out_specs=P(("rep", "tm"), "height", None, None),
        check_vma=False,
    )
```

```python
import functools
import math

import jax
import jax.numpy as jnp
from jax import lax
from jax.experimental import pallas as pl
from jax.experimental.pallas import tpu as pltpu
from jax.sharding import PartitionSpec as P

DH = 128
ZT = 2
LOG2E = 1.4426950408889634


def kernel(
    peers,
    frames_axis,
    heads,
    cells,
    text_rows,
    q_ref,
    k_ref,
    v_ref,
    tk_ref,
    tv_ref,
    len_ref,
    out_ref,
    kv,
    qh,
    oh,
    text,
    text_k,
    text_v,
    text_s,
    scores,
    a2a_send,
    a2a_recv,
    halo_send,
    halo_recv,
    out_send,
    out_recv,
    text_send,
    text_recv,
    local_sem,
):
    me_t = lax.axis_index("tm")
    me_z = lax.axis_index("height")
    tiles = peers // ZT
    nxt = lax.rem(me_t + 1, frames_axis)
    prv = lax.rem(me_t + frames_axis - 1, frames_axis)

    def offset(j):
        return jnp.where(lax.rem(j, 2) == 1, (j + 1) // 2, peers - j // 2)

    def columns(z, h):
        return pl.ds(pl.multiple_of((z * heads + h) * DH, DH), DH)

    barrier = pltpu.get_barrier_semaphore()

    def greet_z(j, c):
        pl.semaphore_signal(barrier, inc=1, device_id={"height": lax.rem(me_z + j, peers)})
        return c

    def greet_t(j, c):
        pl.semaphore_signal(barrier, inc=1, device_id={"tm": lax.rem(me_t + j, frames_axis)})
        return c

    lax.fori_loop(1, peers, greet_z, 0)
    lax.fori_loop(1, frames_axis, greet_t, 0)
    pl.semaphore_wait(barrier, peers - 1 + frames_axis - 1)

    sources = (k_ref, v_ref, q_ref)

    def landing(which, h, z):
        return qh.at[h, z] if which == 2 else kv.at[1, h, z, which]

    def a2a(which, h, d, z):
        return pltpu.make_async_remote_copy(
            src_ref=sources[which].at[:, columns(z, h)],
            dst_ref=landing(which, h, me_z),
            send_sem=a2a_send.at[h, which, d],
            recv_sem=a2a_recv.at[h, which, d],
            device_id={"height": z},
        )

    def arrival(which, h, d, z):
        return pltpu.make_async_remote_copy(
            src_ref=sources[which].at[:, columns(z, h)],
            dst_ref=landing(which, h, z),
            send_sem=a2a_send.at[h, which, d],
            recv_sem=a2a_recv.at[h, which, d],
            device_id={"height": z},
        )

    def own(which, h):
        return pltpu.make_async_copy(
            sources[which].at[:, columns(me_z, h)], landing(which, h, me_z), local_sem.at[h, which]
        )

    def send(which_list, h, d):
        z = lax.rem(me_z + d, peers)
        for which in which_list:
            a2a(which, h, d, z).start()

    def send_all(which_list, h):
        def step(j, c):
            send(which_list, h, offset(j))
            return c

        lax.fori_loop(1, peers, step, 0)

    def halo(h, z, side):
        return pltpu.make_async_remote_copy(
            src_ref=kv.at[1, h, z],
            dst_ref=kv.at[2 * side, h, z],
            send_sem=halo_send.at[h, side, z],
            recv_sem=halo_recv.at[h, side, z],
            device_id={"tm": nxt if side == 0 else prv},
        )

    def forward_own(h):
        for which in range(2):
            own(which, h).wait()
        for side in range(2):
            halo(h, me_z, side).start()

    def forward(h, beside, first, end):
        def step(j, c):
            d = offset(j)
            z = lax.rem(me_z + peers - d, peers)
            beside(j)
            for which in range(2):
                arrival(which, h, d, z).wait_recv()
            for side in range(2):
                halo(h, z, side).start()
            return c

        lax.fori_loop(first, end, step, 0)

    def send_text(j):
        pltpu.make_async_remote_copy(
            src_ref=text.at[me_t],
            dst_ref=text.at[me_t],
            send_sem=text_send,
            recv_sem=text_recv,
            device_id={"tm": lax.rem(me_t + j, frames_axis)},
        ).start()

    share = -(-(frames_axis - 1) // (peers - 1))

    def beside_first(j):
        send((0, 1), 1, offset(j))

        def step(i, c):
            send_text(i)
            return c

        start = 1 + (j - 1) * share
        lax.fori_loop(start, jnp.minimum(start + share, frames_axis), step, 0)

    def beside_last(j):
        pass

    for h in range(heads):
        for which in range(3):
            own(which, h).start()
    send_all((0, 1), 0)
    own_text = [tk_ref[...].astype(jnp.float32), tv_ref[...].astype(jnp.float32)]
    text[me_t] = jnp.concatenate(own_text, 0).astype(jnp.bfloat16)

    def first_queries(j, c):
        send((2,), 0, offset(peers - j))
        return c

    lax.fori_loop(1, peers, first_queries, 0)
    forward_own(0)
    forward(0, beside_first, 1, peers)

    def last_queries(j, c):
        send((2,), 1, offset(peers - j))
        return c

    lax.fori_loop(1, peers, last_queries, 0)
    forward_own(1)

    rest = text.at[pl.ds(1, frames_axis - 1)]
    all_text = pltpu.make_async_remote_copy(
        src_ref=rest, dst_ref=rest, send_sem=text_send, recv_sem=text_recv, device_id={"tm": nxt}
    )
    all_text.wait()
    for h in range(heads):
        both = text[:, :, h * DH : (h + 1) * DH].astype(jnp.float32)
        text_k[h] = both[:, :text_rows].reshape(-1, DH).astype(jnp.bfloat16)
        text_v[h] = both[:, text_rows:].reshape(-1, DH).astype(jnp.bfloat16)

    scale = LOG2E / math.sqrt(DH)
    rows = ZT * cells
    bias = (
        jnp.where(me_t == 0, -jnp.inf, 0.0).astype(jnp.float32),
        jnp.float32(0.0),
        jnp.where(me_t == frames_axis - 1, -jnp.inf, 0.0).astype(jnp.float32),
    )

    def product(q, k):
        return lax.dot_general(q, k, (((1,), (1,)), ((), ())), preferred_element_type=jnp.float32)

    def lanes_max(s):
        parts = [s[:, i : i + DH] for i in range(0, s.shape[1], DH)]
        return functools.reduce(jnp.maximum, parts)

    def weights_of(s, shift):
        parts = [
            jnp.exp2(s[:, i : i + DH] * scale - shift) for i in range(0, s.shape[1], DH)
        ]
        rounded = jnp.concatenate([p.astype(jnp.bfloat16) for p in parts], 1)
        return rounded, functools.reduce(jnp.add, parts)

    def tile(h, a, start, count):
        n = count * cells
        chunks = [(c, min(256, n - c)) for c in range(0, n, 256)]
        wide_chunks = [(0, 512), (512, n - 512)]
        q = qh[h, pl.ds(ZT * a, ZT)].reshape(rows, DH)
        s = product(q, text_k[h])
        place = lax.broadcasted_iota(jnp.int32, s.shape, 1)
        s = jnp.where(place < len_ref[0], s, -jnp.inf)
        text_s[...] = s
        top = lanes_max(s)
        for t in range(3):
            k = kv[t, h, pl.ds(start, count), 0].reshape(n, DH)
            part = None
            for c, w in chunks:
                s = product(q, k[c : c + w])
                scores[t, :, c : c + w] = s
                m = lanes_max(s)
                part = m if part is None else jnp.maximum(part, m)
            top = jnp.maximum(top, part + bias[t])
        top = jnp.broadcast_to(jnp.max(top, 1, keepdims=True) * scale, (rows, DH))

        pieces = [(t, c, w) for t in range(3) for c, w in wide_chunks]
        values = [kv[t, h, pl.ds(start, count), 1].reshape(n, DH) for t in range(3)]
        shifts = [top - b for b in bias]

        def value_product(p, v):
            return jnp.dot(p, v, preferred_element_type=jnp.float32)

        acc = None
        held, total = weights_of(text_s[...], top)
        held_v = text_v[h]
        for t, c, w in pieces:
            p, sums = weights_of(scores[t, :, c : c + w], shifts[t])
            total = total + sums
            part = value_product(held, held_v)
            acc = part if acc is None else acc + part
            held, held_v = p, values[t][c : c + w]
        acc = acc + value_product(held, held_v)
        total = jnp.sum(total, 1, keepdims=True)
        oh[h, pl.ds(ZT * a, ZT)] = (acc / total).astype(jnp.bfloat16).reshape(ZT, cells, DH)

    def result(h, z):
        return pltpu.make_async_remote_copy(
            src_ref=oh.at[h, z],
            dst_ref=out_ref.at[:, columns(me_z, h)],
            send_sem=out_send.at[h, z],
            recv_sem=out_recv.at[h, me_z],
            device_id={"height": z},
        )

    def result_own(h):
        return pltpu.make_async_copy(
            oh.at[h, me_z], out_ref.at[:, columns(me_z, h)], out_send.at[h, me_z]
        )

    def send_tile(h, a):
        for i in range(ZT):
            z = ZT * a + i

            @pl.when(z != me_z)
            def _():
                result(h, z).start()

            @pl.when(z == me_z)
            def _():
                result_own(h).start()

    def wait_queries(h, a):
        for i in range(ZT):
            z = ZT * a + i

            @pl.when(z != me_z)
            def _():
                arrival(2, h, lax.rem(me_z + peers - z, peers), z).wait_recv()

            @pl.when(z == me_z)
            def _():
                own(2, h).wait()

    for h in range(heads):
        def halo_step(z, c, h=h):
            for side in range(2):
                halo(h, z, side).wait_recv()
            return c

        lax.fori_loop(0, peers, halo_step, 0)

        def tile_step(i, c, h=h):
            side = 1 + 2 * lax.rem(me_t, 2)
            ahead = jnp.where(i == 0, 2, jnp.where(i == 1, side, jnp.where(i == 2, 4 - side, 0)))
            a = lax.rem(me_z // ZT + ahead, tiles)
            low = a == 0
            at_edge = jnp.logical_or(low, a == tiles - 1)
            wait_queries(h, a)

            @pl.when(at_edge)
            def _():
                tile(h, a, jnp.where(low, 0, (tiles - 2) * ZT), 2 * ZT)

            @pl.when(jnp.logical_not(at_edge))
            def _():
                tile(h, a, (a - 1) * ZT, 3 * ZT)

            send_tile(h, a)
            if h == 0:
                begin = 1 + 3 * i
                forward(1, beside_last, begin, jnp.minimum(begin + 3, peers))
            return c

        lax.fori_loop(0, tiles, tile_step, 0)

    for h in range(heads):
        result_own(h).wait()

        def end_step(j, c, h=h):
            d = offset(j)
            z = lax.rem(me_z + d, peers)
            for which in range(3):
                a2a(which, h, d, z).wait_send()
            result(h, z).wait_send()
            pltpu.make_async_remote_copy(
                src_ref=oh.at[h, z],
                dst_ref=out_ref.at[:, columns(z, h)],
                send_sem=out_send.at[h, z],
                recv_sem=out_recv.at[h, z],
                device_id={"height": z},
            ).wait_recv()
            return c

        lax.fori_loop(1, peers, end_step, 0)

        def halo_end(z, c, h=h):
            for side in range(2):
                halo(h, z, side).wait_send()
            return c

        lax.fori_loop(0, peers, halo_end, 0)


def per_device(queries, key_tokens, value_tokens, text_keys, text_values, text_length):
    shape = queries.shape
    features = shape[3]
    cells = shape[0] * shape[1] * shape[2]
    peers = lax.axis_size("height")
    frames_axis = lax.axis_size("tm")
    heads = features // DH // peers
    text_rows = text_keys.shape[0]
    flat = [x.reshape(cells, features) for x in (queries, key_tokens, value_tokens)]
    any_space = pl.BlockSpec(memory_space=pl.ANY)
    vmem = pl.BlockSpec(memory_space=pltpu.VMEM)
    dma = pltpu.SemaphoreType.DMA
    result = pl.pallas_call(
        functools.partial(kernel, peers, frames_axis, heads, cells, text_rows),
        out_shape=jax.ShapeDtypeStruct((cells, features), jnp.bfloat16),
        in_specs=[any_space] * 3 + [vmem] * 2 + [pl.BlockSpec(memory_space=pltpu.SMEM)],
        out_specs=any_space,
        scratch_shapes=[
            pltpu.VMEM((3, heads, peers, 2, cells, DH), jnp.bfloat16),
            pltpu.VMEM((heads, peers, cells, DH), jnp.bfloat16),
            pltpu.VMEM((heads, peers, cells, DH), jnp.bfloat16),
            pltpu.VMEM((frames_axis, 2 * text_rows, heads * DH), jnp.bfloat16),
            pltpu.VMEM((heads, frames_axis * text_rows, DH), jnp.bfloat16),
            pltpu.VMEM((heads, frames_axis * text_rows, DH), jnp.bfloat16),
            pltpu.VMEM((ZT * cells, frames_axis * text_rows), jnp.float32),
            pltpu.VMEM((3, ZT * cells, 3 * ZT * cells), jnp.float32),
            dma((heads, 3, peers)),
            dma((heads, 3, peers)),
            dma((heads, 2, peers)),
            dma((heads, 2, peers)),
            dma((heads, peers)),
            dma((heads, peers)),
            dma,
            dma,
            dma((heads, 3)),
        ],
        compiler_params=pltpu.CompilerParams(
            collective_id=0, has_side_effects=True, vmem_limit_bytes=62 * 1024 * 1024
        ),
        cost_estimate=pl.CostEstimate(
            flops=5_000_000_000, bytes_accessed=4_000_000, transcendentals=10_000_000
        ),
    )(*flat, text_keys, text_values, text_length)
    return result.reshape(shape)


def solution(mesh):
    placed = (
        P(("rep", "tm"), "height", None, None),
        P(("rep", "tm"), "height", None, None),
        P(("rep", "tm"), "height", None, None),
        P(("rep", "tm"), "height"),
        P(("rep", "tm"), "height"),
        P("rep"),
    )
    return jax.shard_map(
        per_device,
        mesh=mesh,
        in_specs=placed,
        out_specs=P(("rep", "tm"), "height", None, None),
        check_vma=False,
    )
```

```python
import functools
import math

import jax
import jax.numpy as jnp
from jax import lax
from jax.experimental import pallas as pl
from jax.experimental.pallas import tpu as pltpu
from jax.sharding import PartitionSpec as P

DH = 128
ZT = 2
LOG2E = 1.4426950408889634


def kernel(
    peers,
    frames_axis,
    heads,
    cells,
    text_rows,
    q_ref,
    k_ref,
    v_ref,
    tk_ref,
    tv_ref,
    len_ref,
    out_ref,
    kv,
    qh,
    oh,
    text,
    text_k,
    text_v,
    text_s,
    scores,
    a2a_send,
    a2a_recv,
    halo_send,
    halo_recv,
    out_send,
    out_recv,
    text_send,
    text_recv,
    local_sem,
):
    me_t = lax.axis_index("tm")
    me_z = lax.axis_index("height")
    tiles = peers // ZT
    nxt = lax.rem(me_t + 1, frames_axis)
    prv = lax.rem(me_t + frames_axis - 1, frames_axis)

    def offset(j):
        return jnp.where(lax.rem(j, 2) == 1, (j + 1) // 2, peers - j // 2)

    def columns(z, h):
        return pl.ds(pl.multiple_of((z * heads + h) * DH, DH), DH)

    barrier = pltpu.get_barrier_semaphore()

    def greet_z(j, c):
        pl.semaphore_signal(barrier, inc=1, device_id={"height": lax.rem(me_z + j, peers)})
        return c

    def greet_t(j, c):
        pl.semaphore_signal(barrier, inc=1, device_id={"tm": lax.rem(me_t + j, frames_axis)})
        return c

    lax.fori_loop(1, peers, greet_z, 0)
    lax.fori_loop(1, frames_axis, greet_t, 0)
    pl.semaphore_wait(barrier, peers - 1 + frames_axis - 1)

    sources = (k_ref, v_ref, q_ref)

    def landing(which, h, z):
        return qh.at[h, z] if which == 2 else kv.at[1, h, z, which]

    def a2a(which, h, d, z):
        return pltpu.make_async_remote_copy(
            src_ref=sources[which].at[:, columns(z, h)],
            dst_ref=landing(which, h, me_z),
            send_sem=a2a_send.at[h, which, d],
            recv_sem=a2a_recv.at[h, which, d],
            device_id={"height": z},
        )

    def arrival(which, h, d, z):
        return pltpu.make_async_remote_copy(
            src_ref=sources[which].at[:, columns(z, h)],
            dst_ref=landing(which, h, z),
            send_sem=a2a_send.at[h, which, d],
            recv_sem=a2a_recv.at[h, which, d],
            device_id={"height": z},
        )

    def own(which, h):
        return pltpu.make_async_copy(
            sources[which].at[:, columns(me_z, h)], landing(which, h, me_z), local_sem.at[h, which]
        )

    def send(which_list, h, d):
        z = lax.rem(me_z + d, peers)
        for which in which_list:
            a2a(which, h, d, z).start()

    def send_all(which_list, h):
        def step(j, c):
            send(which_list, h, offset(j))
            return c

        lax.fori_loop(1, peers, step, 0)

    def halo(h, z, side):
        return pltpu.make_async_remote_copy(
            src_ref=kv.at[1, h, z],
            dst_ref=kv.at[2 * side, h, z],
            send_sem=halo_send.at[h, side, z],
            recv_sem=halo_recv.at[h, side, z],
            device_id={"tm": nxt if side == 0 else prv},
        )

    def forward_own(h):
        for which in range(2):
            own(which, h).wait()
        for side in range(2):
            halo(h, me_z, side).start()

    def forward(h, beside, first, end):
        def step(j, c):
            d = offset(j)
            z = lax.rem(me_z + peers - d, peers)
            beside(j)
            for which in range(2):
                arrival(which, h, d, z).wait_recv()
            for side in range(2):
                halo(h, z, side).start()
            return c

        lax.fori_loop(first, end, step, 0)

    def send_text(j):
        pltpu.make_async_remote_copy(
            src_ref=text.at[me_t],
            dst_ref=text.at[me_t],
            send_sem=text_send,
            recv_sem=text_recv,
            device_id={"tm": lax.rem(me_t + j, frames_axis)},
        ).start()

    share = -(-(frames_axis - 1) // (peers - 1))

    def beside_first(j):
        send((0, 1), 1, offset(j))

        def step(i, c):
            send_text(i)
            return c

        start = 1 + (j - 1) * share
        lax.fori_loop(start, jnp.minimum(start + share, frames_axis), step, 0)

    def beside_last(j):
        pass

    for h in range(heads):
        for which in range(3):
            own(which, h).start()
    send_all((0, 1), 0)
    own_text = [tk_ref[...].astype(jnp.float32), tv_ref[...].astype(jnp.float32)]
    text[me_t] = jnp.concatenate(own_text, 0).astype(jnp.bfloat16)

    def first_queries(j, c):
        send((2,), 0, offset(peers - j))
        return c

    lax.fori_loop(1, peers, first_queries, 0)
    forward_own(0)
    forward(0, beside_first, 1, peers)

    def last_queries(j, c):
        send((2,), 1, offset(peers - j))
        return c

    lax.fori_loop(1, peers, last_queries, 0)
    forward_own(1)

    rest = text.at[pl.ds(1, frames_axis - 1)]
    all_text = pltpu.make_async_remote_copy(
        src_ref=rest, dst_ref=rest, send_sem=text_send, recv_sem=text_recv, device_id={"tm": nxt}
    )
    all_text.wait()
    for h in range(heads):
        both = text[:, :, h * DH : (h + 1) * DH].astype(jnp.float32)
        text_k[h] = both[:, :text_rows].reshape(-1, DH).astype(jnp.bfloat16)
        text_v[h] = both[:, text_rows:].reshape(-1, DH).astype(jnp.bfloat16)

    scale = LOG2E / math.sqrt(DH)
    rows = ZT * cells
    bias = (
        jnp.where(me_t == 0, -jnp.inf, 0.0).astype(jnp.float32),
        jnp.float32(0.0),
        jnp.where(me_t == frames_axis - 1, -jnp.inf, 0.0).astype(jnp.float32),
    )

    def product(q, k):
        return lax.dot_general(q, k, (((1,), (1,)), ((), ())), preferred_element_type=jnp.float32)

    def lanes_max(s):
        parts = [s[:, i : i + DH] for i in range(0, s.shape[1], DH)]
        return functools.reduce(jnp.maximum, parts)

    def weights_of(s, shift):
        parts = [
            jnp.exp2(s[:, i : i + DH] * scale - shift) for i in range(0, s.shape[1], DH)
        ]
        rounded = jnp.concatenate([p.astype(jnp.bfloat16) for p in parts], 1)
        return rounded, functools.reduce(jnp.add, parts)

    def tile(h, a, start, count):
        n = count * cells
        q = qh[h, pl.ds(ZT * a, ZT)].reshape(rows, DH)
        s = product(q, text_k[h])
        place = lax.broadcasted_iota(jnp.int32, s.shape, 1)
        s = jnp.where(place < len_ref[0], s, -jnp.inf)
        text_s[...] = s
        top = lanes_max(s)
        for t in range(3):
            k = kv[t, h, pl.ds(start, count), 0].reshape(n, DH)
            s = product(q, k)
            scores[t, :, :n] = s
            top = jnp.maximum(top, lanes_max(s) + bias[t])
        top = jnp.broadcast_to(jnp.max(top, 1, keepdims=True) * scale, (rows, DH))

        values = [kv[t, h, pl.ds(start, count), 1].reshape(n, DH) for t in range(3)]
        shifts = [top - b for b in bias]

        def value_product(p, v):
            return jnp.dot(p, v, preferred_element_type=jnp.float32)

        acc = None
        held, total = weights_of(text_s[...], top)
        held_v = text_v[h]
        for t in range(3):
            p, sums = weights_of(scores[t, :, :n], shifts[t])
            total = total + sums
            part = value_product(held, held_v)
            acc = part if acc is None else acc + part
            held, held_v = p, values[t]
        acc = acc + value_product(held, held_v)
        total = jnp.sum(total, 1, keepdims=True)
        oh[h, pl.ds(ZT * a, ZT)] = (acc / total).astype(jnp.bfloat16).reshape(ZT, cells, DH)

    def result(h, z):
        return pltpu.make_async_remote_copy(
            src_ref=oh.at[h, z],
            dst_ref=out_ref.at[:, columns(me_z, h)],
            send_sem=out_send.at[h, z],
            recv_sem=out_recv.at[h, me_z],
            device_id={"height": z},
        )

    def result_own(h):
        return pltpu.make_async_copy(
            oh.at[h, me_z], out_ref.at[:, columns(me_z, h)], out_send.at[h, me_z]
        )

    def send_tile(h, a):
        for i in range(ZT):
            z = ZT * a + i

            @pl.when(z != me_z)
            def _():
                result(h, z).start()

            @pl.when(z == me_z)
            def _():
                result_own(h).start()

    def wait_queries(h, a):
        for i in range(ZT):
            z = ZT * a + i

            @pl.when(z != me_z)
            def _():
                arrival(2, h, lax.rem(me_z + peers - z, peers), z).wait_recv()

            @pl.when(z == me_z)
            def _():
                own(2, h).wait()

    for h in range(heads):
        def halo_step(z, c, h=h):
            for side in range(2):
                halo(h, z, side).wait_recv()
            return c

        lax.fori_loop(0, peers, halo_step, 0)

        def tile_step(i, c, h=h):
            side = 1 + 2 * lax.rem(me_t, 2)
            ahead = jnp.where(i == 0, 2, jnp.where(i == 1, side, jnp.where(i == 2, 4 - side, 0)))
            a = lax.rem(me_z // ZT + ahead, tiles)
            low = a == 0
            at_edge = jnp.logical_or(low, a == tiles - 1)
            wait_queries(h, a)

            @pl.when(at_edge)
            def _():
                tile(h, a, jnp.where(low, 0, (tiles - 2) * ZT), 2 * ZT)

            @pl.when(jnp.logical_not(at_edge))
            def _():
                tile(h, a, (a - 1) * ZT, 3 * ZT)

            send_tile(h, a)
            if h == 0:
                begin = 1 + 3 * i
                forward(1, beside_last, begin, jnp.minimum(begin + 3, peers))
            return c

        lax.fori_loop(0, tiles, tile_step, 0)

    for h in range(heads):
        result_own(h).wait()

        def end_step(j, c, h=h):
            d = offset(j)
            z = lax.rem(me_z + d, peers)
            for which in range(3):
                a2a(which, h, d, z).wait_send()
            result(h, z).wait_send()
            pltpu.make_async_remote_copy(
                src_ref=oh.at[h, z],
                dst_ref=out_ref.at[:, columns(z, h)],
                send_sem=out_send.at[h, z],
                recv_sem=out_recv.at[h, z],
                device_id={"height": z},
            ).wait_recv()
            return c

        lax.fori_loop(1, peers, end_step, 0)

        def halo_end(z, c, h=h):
            for side in range(2):
                halo(h, z, side).wait_send()
            return c

        lax.fori_loop(0, peers, halo_end, 0)


def per_device(queries, key_tokens, value_tokens, text_keys, text_values, text_length):
    shape = queries.shape
    features = shape[3]
    cells = shape[0] * shape[1] * shape[2]
    peers = lax.axis_size("height")
    frames_axis = lax.axis_size("tm")
    heads = features // DH // peers
    text_rows = text_keys.shape[0]
    flat = [x.reshape(cells, features) for x in (queries, key_tokens, value_tokens)]
    any_space = pl.BlockSpec(memory_space=pl.ANY)
    vmem = pl.BlockSpec(memory_space=pltpu.VMEM)
    dma = pltpu.SemaphoreType.DMA
    result = pl.pallas_call(
        functools.partial(kernel, peers, frames_axis, heads, cells, text_rows),
        out_shape=jax.ShapeDtypeStruct((cells, features), jnp.bfloat16),
        in_specs=[any_space] * 3 + [vmem] * 2 + [pl.BlockSpec(memory_space=pltpu.SMEM)],
        out_specs=any_space,
        scratch_shapes=[
            pltpu.VMEM((3, heads, peers, 2, cells, DH), jnp.bfloat16),
            pltpu.VMEM((heads, peers, cells, DH), jnp.bfloat16),
            pltpu.VMEM((heads, peers, cells, DH), jnp.bfloat16),
            pltpu.VMEM((frames_axis, 2 * text_rows, heads * DH), jnp.bfloat16),
            pltpu.VMEM((heads, frames_axis * text_rows, DH), jnp.bfloat16),
            pltpu.VMEM((heads, frames_axis * text_rows, DH), jnp.bfloat16),
            pltpu.VMEM((ZT * cells, frames_axis * text_rows), jnp.float32),
            pltpu.VMEM((3, ZT * cells, 3 * ZT * cells), jnp.float32),
            dma((heads, 3, peers)),
            dma((heads, 3, peers)),
            dma((heads, 2, peers)),
            dma((heads, 2, peers)),
            dma((heads, peers)),
            dma((heads, peers)),
            dma,
            dma,
            dma((heads, 3)),
        ],
        compiler_params=pltpu.CompilerParams(
            collective_id=0, has_side_effects=True, vmem_limit_bytes=62 * 1024 * 1024
        ),
        cost_estimate=pl.CostEstimate(
            flops=5_000_000_000, bytes_accessed=4_000_000, transcendentals=10_000_000
        ),
    )(*flat, text_keys, text_values, text_length)
    return result.reshape(shape)


def solution(mesh):
    placed = (
        P(("rep", "tm"), "height", None, None),
        P(("rep", "tm"), "height", None, None),
        P(("rep", "tm"), "height", None, None),
        P(("rep", "tm"), "height"),
        P(("rep", "tm"), "height"),
        P("rep"),
    )
    return jax.shard_map(
        per_device,
        mesh=mesh,
        in_specs=placed,
        out_specs=P(("rep", "tm"), "height", None, None),
        check_vma=False,
    )
```

```python
import functools
import math

import jax
import jax.numpy as jnp
from jax import lax
from jax.experimental import pallas as pl
from jax.experimental.pallas import tpu as pltpu
from jax.sharding import PartitionSpec as P

DH = 128
ZT = 2
LOG2E = 1.4426950408889634


def kernel(
    peers,
    frames_axis,
    heads,
    cells,
    text_rows,
    q_ref,
    k_ref,
    v_ref,
    tk_ref,
    tv_ref,
    len_ref,
    out_ref,
    kv,
    qh,
    oh,
    text,
    text_k,
    text_v,
    text_s,
    scores,
    a2a_send,
    a2a_recv,
    halo_send,
    halo_recv,
    out_send,
    out_recv,
    text_send,
    text_recv,
    local_sem,
):
    me_t = lax.axis_index("tm")
    me_z = lax.axis_index("height")
    tiles = peers // ZT
    nxt = lax.rem(me_t + 1, frames_axis)
    prv = lax.rem(me_t + frames_axis - 1, frames_axis)

    def offset(j):
        d = jnp.where(lax.rem(j, 2) == 1, (j + 1) // 2, peers - j // 2)
        return jnp.where(lax.rem(me_t, 2) == 0, d, peers - d)

    def columns(z, h):
        return pl.ds(pl.multiple_of((z * heads + h) * DH, DH), DH)

    barrier = pltpu.get_barrier_semaphore()

    def greet_z(j, c):
        pl.semaphore_signal(barrier, inc=1, device_id={"height": lax.rem(me_z + j, peers)})
        return c

    def greet_t(j, c):
        pl.semaphore_signal(barrier, inc=1, device_id={"tm": lax.rem(me_t + j, frames_axis)})
        return c

    lax.fori_loop(1, peers, greet_z, 0)
    lax.fori_loop(1, frames_axis, greet_t, 0)
    pl.semaphore_wait(barrier, peers - 1 + frames_axis - 1)

    sources = (k_ref, v_ref, q_ref)

    def landing(which, h, z):
        return qh.at[h, z] if which == 2 else kv.at[1, h, z, which]

    def a2a(which, h, d, z):
        return pltpu.make_async_remote_copy(
            src_ref=sources[which].at[:, columns(z, h)],
            dst_ref=landing(which, h, me_z),
            send_sem=a2a_send.at[h, which, d],
            recv_sem=a2a_recv.at[h, which, d],
            device_id={"height": z},
        )

    def arrival(which, h, d, z):
        return pltpu.make_async_remote_copy(
            src_ref=sources[which].at[:, columns(z, h)],
            dst_ref=landing(which, h, z),
            send_sem=a2a_send.at[h, which, d],
            recv_sem=a2a_recv.at[h, which, d],
            device_id={"height": z},
        )

    def own(which, h):
        return pltpu.make_async_copy(
            sources[which].at[:, columns(me_z, h)], landing(which, h, me_z), local_sem.at[h, which]
        )

    def send(which_list, h, d):
        z = lax.rem(me_z + d, peers)
        for which in which_list:
            a2a(which, h, d, z).start()

    def send_all(which_list, h):
        def step(j, c):
            send(which_list, h, offset(j))
            return c

        lax.fori_loop(1, peers, step, 0)

    def halo(h, z, side):
        return pltpu.make_async_remote_copy(
            src_ref=kv.at[1, h, z],
            dst_ref=kv.at[2 * side, h, z],
            send_sem=halo_send.at[h, side, z],
            recv_sem=halo_recv.at[h, side, z],
            device_id={"tm": nxt if side == 0 else prv},
        )

    def forward_own(h):
        for which in range(2):
            own(which, h).wait()
        for side in range(2):
            halo(h, me_z, side).start()

    def forward(h, beside, first, end):
        def step(j, c):
            d = offset(j)
            z = lax.rem(me_z + peers - d, peers)
            beside(j)
            for which in range(2):
                arrival(which, h, d, z).wait_recv()
            for side in range(2):
                halo(h, z, side).start()
            return c

        lax.fori_loop(first, end, step, 0)

    def send_text(j):
        pltpu.make_async_remote_copy(
            src_ref=text.at[me_t],
            dst_ref=text.at[me_t],
            send_sem=text_send,
            recv_sem=text_recv,
            device_id={"tm": lax.rem(me_t + j, frames_axis)},
        ).start()

    share = -(-(frames_axis - 1) // (peers - 1))

    def beside_first(j):
        send((0, 1), 1, offset(j))

        def step(i, c):
            send_text(i)
            return c

        start = 1 + (j - 1) * share
        lax.fori_loop(start, jnp.minimum(start + share, frames_axis), step, 0)

    def beside_last(j):
        pass

    for h in range(heads):
        for which in range(3):
            own(which, h).start()
    send_all((0, 1), 0)
    own_text = [tk_ref[...].astype(jnp.float32), tv_ref[...].astype(jnp.float32)]
    text[me_t] = jnp.concatenate(own_text, 0).astype(jnp.bfloat16)

    def first_queries(j, c):
        send((2,), 0, offset(peers - j))
        return c

    lax.fori_loop(1, peers, first_queries, 0)
    forward_own(0)
    forward(0, beside_first, 1, peers)

    def last_queries(j, c):
        send((2,), 1, offset(peers - j))
        return c

    lax.fori_loop(1, peers, last_queries, 0)
    forward_own(1)

    rest = text.at[pl.ds(1, frames_axis - 1)]
    all_text = pltpu.make_async_remote_copy(
        src_ref=rest, dst_ref=rest, send_sem=text_send, recv_sem=text_recv, device_id={"tm": nxt}
    )
    all_text.wait()
    for h in range(heads):
        both = text[:, :, h * DH : (h + 1) * DH].astype(jnp.float32)
        text_k[h] = both[:, :text_rows].reshape(-1, DH).astype(jnp.bfloat16)
        text_v[h] = both[:, text_rows:].reshape(-1, DH).astype(jnp.bfloat16)

    scale = LOG2E / math.sqrt(DH)
    rows = ZT * cells
    bias = (
        jnp.where(me_t == 0, -jnp.inf, 0.0).astype(jnp.float32),
        jnp.float32(0.0),
        jnp.where(me_t == frames_axis - 1, -jnp.inf, 0.0).astype(jnp.float32),
    )

    def product(q, k):
        return lax.dot_general(q, k, (((1,), (1,)), ((), ())), preferred_element_type=jnp.float32)

    def lanes_max(s):
        parts = [s[:, i : i + DH] for i in range(0, s.shape[1], DH)]
        return functools.reduce(jnp.maximum, parts)

    def weights_of(s, shift):
        parts = [
            jnp.exp2(s[:, i : i + DH] * scale - shift) for i in range(0, s.shape[1], DH)
        ]
        rounded = jnp.concatenate([p.astype(jnp.bfloat16) for p in parts], 1)
        return rounded, functools.reduce(jnp.add, parts)

    def tile(h, a, start, count):
        n = count * cells
        q = qh[h, pl.ds(ZT * a, ZT)].reshape(rows, DH)
        s = product(q, text_k[h])
        place = lax.broadcasted_iota(jnp.int32, s.shape, 1)
        s = jnp.where(place < len_ref[0], s, -jnp.inf)
        text_s[...] = s
        top = lanes_max(s)
        for t in range(3):
            k = kv[t, h, pl.ds(start, count), 0].reshape(n, DH)
            s = product(q, k)
            scores[t, :, :n] = s
            top = jnp.maximum(top, lanes_max(s) + bias[t])
        top = jnp.broadcast_to(jnp.max(top, 1, keepdims=True) * scale, (rows, DH))

        values = [kv[t, h, pl.ds(start, count), 1].reshape(n, DH) for t in range(3)]
        shifts = [top - b for b in bias]

        def value_product(p, v):
            return jnp.dot(p, v, preferred_element_type=jnp.float32)

        acc = None
        held, total = weights_of(text_s[...], top)
        held_v = text_v[h]
        for t in range(3):
            p, sums = weights_of(scores[t, :, :n], shifts[t])
            total = total + sums
            part = value_product(held, held_v)
            acc = part if acc is None else acc + part
            held, held_v = p, values[t]
        acc = acc + value_product(held, held_v)
        total = jnp.sum(total, 1, keepdims=True)
        oh[h, pl.ds(ZT * a, ZT)] = (acc / total).astype(jnp.bfloat16).reshape(ZT, cells, DH)

    def result(h, z):
        return pltpu.make_async_remote_copy(
            src_ref=oh.at[h, z],
            dst_ref=out_ref.at[:, columns(me_z, h)],
            send_sem=out_send.at[h, z],
            recv_sem=out_recv.at[h, me_z],
            device_id={"height": z},
        )

    def result_own(h):
        return pltpu.make_async_copy(
            oh.at[h, me_z], out_ref.at[:, columns(me_z, h)], out_send.at[h, me_z]
        )

    def send_tile(h, a):
        for i in range(ZT):
            z = ZT * a + i

            @pl.when(z != me_z)
            def _():
                result(h, z).start()

            @pl.when(z == me_z)
            def _():
                result_own(h).start()

    def wait_queries(h, a):
        for i in range(ZT):
            z = ZT * a + i

            @pl.when(z != me_z)
            def _():
                arrival(2, h, lax.rem(me_z + peers - z, peers), z).wait_recv()

            @pl.when(z == me_z)
            def _():
                own(2, h).wait()

    for h in range(heads):
        def halo_step(z, c, h=h):
            for side in range(2):
                halo(h, z, side).wait_recv()
            return c

        lax.fori_loop(0, peers, halo_step, 0)

        def tile_step(i, c, h=h):
            side = 1 + 2 * lax.rem(me_t, 2)
            ahead = jnp.where(i == 0, 2, jnp.where(i == 1, side, jnp.where(i == 2, 4 - side, 0)))
            a = lax.rem(me_z // ZT + ahead, tiles)
            low = a == 0
            at_edge = jnp.logical_or(low, a == tiles - 1)
            wait_queries(h, a)

            @pl.when(at_edge)
            def _():
                tile(h, a, jnp.where(low, 0, (tiles - 2) * ZT), 2 * ZT)

            @pl.when(jnp.logical_not(at_edge))
            def _():
                tile(h, a, (a - 1) * ZT, 3 * ZT)

            send_tile(h, a)
            if h == 0:
                begin = 1 + 3 * i
                forward(1, beside_last, begin, jnp.minimum(begin + 3, peers))
            return c

        lax.fori_loop(0, tiles, tile_step, 0)

    for h in range(heads):
        result_own(h).wait()

        def end_step(j, c, h=h):
            d = offset(j)
            z = lax.rem(me_z + d, peers)
            for which in range(3):
                a2a(which, h, d, z).wait_send()
            result(h, z).wait_send()
            pltpu.make_async_remote_copy(
                src_ref=oh.at[h, z],
                dst_ref=out_ref.at[:, columns(z, h)],
                send_sem=out_send.at[h, z],
                recv_sem=out_recv.at[h, z],
                device_id={"height": z},
            ).wait_recv()
            return c

        lax.fori_loop(1, peers, end_step, 0)

        def halo_end(z, c, h=h):
            for side in range(2):
                halo(h, z, side).wait_send()
            return c

        lax.fori_loop(0, peers, halo_end, 0)


def per_device(queries, key_tokens, value_tokens, text_keys, text_values, text_length):
    shape = queries.shape
    features = shape[3]
    cells = shape[0] * shape[1] * shape[2]
    peers = lax.axis_size("height")
    frames_axis = lax.axis_size("tm")
    heads = features // DH // peers
    text_rows = text_keys.shape[0]
    flat = [x.reshape(cells, features) for x in (queries, key_tokens, value_tokens)]
    any_space = pl.BlockSpec(memory_space=pl.ANY)
    vmem = pl.BlockSpec(memory_space=pltpu.VMEM)
    dma = pltpu.SemaphoreType.DMA
    result = pl.pallas_call(
        functools.partial(kernel, peers, frames_axis, heads, cells, text_rows),
        out_shape=jax.ShapeDtypeStruct((cells, features), jnp.bfloat16),
        in_specs=[any_space] * 3 + [vmem] * 2 + [pl.BlockSpec(memory_space=pltpu.SMEM)],
        out_specs=any_space,
        scratch_shapes=[
            pltpu.VMEM((3, heads, peers, 2, cells, DH), jnp.bfloat16),
            pltpu.VMEM((heads, peers, cells, DH), jnp.bfloat16),
            pltpu.VMEM((heads, peers, cells, DH), jnp.bfloat16),
            pltpu.VMEM((frames_axis, 2 * text_rows, heads * DH), jnp.bfloat16),
            pltpu.VMEM((heads, frames_axis * text_rows, DH), jnp.bfloat16),
            pltpu.VMEM((heads, frames_axis * text_rows, DH), jnp.bfloat16),
            pltpu.VMEM((ZT * cells, frames_axis * text_rows), jnp.float32),
            pltpu.VMEM((3, ZT * cells, 3 * ZT * cells), jnp.float32),
            dma((heads, 3, peers)),
            dma((heads, 3, peers)),
            dma((heads, 2, peers)),
            dma((heads, 2, peers)),
            dma((heads, peers)),
            dma((heads, peers)),
            dma,
            dma,
            dma((heads, 3)),
        ],
        compiler_params=pltpu.CompilerParams(
            collective_id=0, has_side_effects=True, vmem_limit_bytes=62 * 1024 * 1024
        ),
        cost_estimate=pl.CostEstimate(
            flops=5_000_000_000, bytes_accessed=4_000_000, transcendentals=10_000_000
        ),
    )(*flat, text_keys, text_values, text_length)
    return result.reshape(shape)


def solution(mesh):
    placed = (
        P(("rep", "tm"), "height", None, None),
        P(("rep", "tm"), "height", None, None),
        P(("rep", "tm"), "height", None, None),
        P(("rep", "tm"), "height"),
        P(("rep", "tm"), "height"),
        P("rep"),
    )
    return jax.shard_map(
        per_device,
        mesh=mesh,
        in_specs=placed,
        out_specs=P(("rep", "tm"), "height", None, None),
        check_vma=False,
    )
```
